256 devices in a mesh: blk: 32 (over z, x_hi, core), head: 8 (over y, x_lo).
Axes of the slice: x: 4 (x_hi: 2, x_lo: 2; x = x_hi * 2 + x_lo), y: 4, z: 8, core: 2. Of those that a mesh axis runs over, the one named last changes fastest.
Arguments:
- queries: bfloat16 [4096, 8192], P('blk', 'head'), may hold values from -6 to 6
- cached_prompt_keys: bfloat16 [16384, 1024], P('blk', 'head'), may hold values from -12 to 12
- cached_prompt_values: bfloat16 [16384, 1024], P('blk', 'head'), may hold values from -6 to 6
- rotated_response_keys: bfloat16 [4096, 1024], P('blk', 'head'), may hold values from -21 to 21
- packed_response_values: bfloat16 [4096, 1024], P('blk', 'head'), may hold values from -6 to 6
- segment_ids: int32 [4096], replicated, may hold values from 0 to 94, as said below
- out_weight: bfloat16 [8192, 8192], P('head', 'blk'), may hold values from -0.5 to 0.5
Outputs:
- attended: bfloat16 [4096, 8192], P('blk', 'head')
The draws below stay inside these ranges and needn't reach their ends.
Inputs may be any that keep to these rules, and one draw needn't show every extreme that they name: `segment_ids`: starts at 0 and never falls along the rows, rising by at most one from row to row; every response has 1 to 128 consecutive rows, one exactly 128; a new response never begins at row k * 128 for k > 0. Each aligned run of 64 rows holds exactly one response start besides its first row, except the two runs that meet at row 128.
All inputs are finite; a program needn't handle non-finite values.
Results may differ from the reference program's by a relative error of at most 0.019.
Values may be sent and summed in bfloat16 or wider, within the bound.
A program may use at most 64 MiB of HBM per device.

```python
import math
import jax
import jax.numpy as jnp
from jax import lax

D = 8192
QUERY_HEADS = 64
KEY_VALUE_HEADS = 8
HEAD_WIDTH = 128
RB = 128
RESP_MAX = 128
RESPONSE_ROWS = 4096
PROMPT_LENGTH = 16384


def draw_queries(key, part):
    key = jax.random.fold_in(key, 3)
    value_rows = jnp.clip(jax.random.normal(key, (RESPONSE_ROWS, QUERY_HEADS * HEAD_WIDTH), jnp.float32), -6.0, 6.0)
    return value_rows.astype(jnp.bfloat16)


def draw_cached_prompt_keys(key, part):
    key = jax.random.fold_in(key, 5)
    value_rows = 2.0 * jnp.clip(jax.random.normal(key, (PROMPT_LENGTH, KEY_VALUE_HEADS * HEAD_WIDTH), jnp.float32), -6.0, 6.0)
    return value_rows.astype(jnp.bfloat16)


def draw_segment_ids(key, part):
    key = jax.random.fold_in(key, 9)
    half_most = RESP_MAX // 2
    window_count = RESPONSE_ROWS // half_most
    row_ids = jnp.arange(RESPONSE_ROWS, dtype=jnp.int32)
    offsets = row_ids % RB
    windows = row_ids // half_most
    inner = row_ids % half_most
    picks = jax.random.randint(key, (window_count,), 1, half_most)
    quiet = (row_ids >= RB - half_most) & (row_ids < RB + half_most)
    extra = (inner == picks[windows]) & jnp.logical_not(quiet)
    first = (inner == 0) & ((offsets != 0) | (row_ids == 0))
    starts = first | extra
    return (jnp.cumsum(starts.astype(jnp.int32)) - 1).astype(jnp.int32)


def steps_of(stream_key, shape, cuts, smallest, high):
    level, own = 1.0, jax.random.fold_in(stream_key, 6)
    for position, parts in cuts:
        steps = jnp.exp(jax.random.uniform(jax.random.fold_in(own, position), (parts,), jnp.float32, smallest / len(cuts), high / len(cuts)))
        level = level * jnp.repeat(steps, shape[position] // parts).reshape([-1 if axis == position else 1 for axis in range(len(shape))])
    return level


def centred(key, extent, spread, limit, split=(), kind=jnp.bfloat16):
    level = steps_of(key, extent, split, -0.22, 0.18) if split else 1.0
    values = jax.random.normal(key, extent, jnp.float32) * spread * level
    return jnp.minimum(jnp.maximum(values, -limit), limit).astype(kind)


def setup_inputs(seed: int = 0) -> dict:
    seeds = jax.random.split(jax.random.key(seed), 8)
    return {
        "queries": draw_queries(jax.random.fold_in(seeds[7], 71), 0),
        "cached_prompt_keys": draw_cached_prompt_keys(jax.random.fold_in(seeds[7], 71), 0),
        "cached_prompt_values": centred(seeds[2], (PROMPT_LENGTH, KEY_VALUE_HEADS * HEAD_WIDTH), 1.0, 6.0, ((0, 32), (1, 8))),
        "rotated_response_keys": centred(seeds[3], (RESPONSE_ROWS, KEY_VALUE_HEADS * HEAD_WIDTH), 3.5, 21.0, ((0, 32), (1, 8))),
        "packed_response_values": centred(seeds[4], (RESPONSE_ROWS, KEY_VALUE_HEADS * HEAD_WIDTH), 1.0, 6.0, ((0, 32), (1, 8))),
        "segment_ids": draw_segment_ids(jax.random.fold_in(seeds[7], 71), 0),
        "out_weight": centred(seeds[6], (QUERY_HEADS * HEAD_WIDTH, D), HEAD_WIDTH ** -0.5, 0.5, ((0, 8), (1, 32))),
    }


def reference(queries, cached_prompt_keys, cached_prompt_values, rotated_response_keys, packed_response_values, segment_ids, out_weight):
    group_width = QUERY_HEADS // KEY_VALUE_HEADS
    score_scale = 1.0 / math.sqrt(HEAD_WIDTH)
    prompt_key_rows = cached_prompt_keys.astype(jnp.float32).reshape(PROMPT_LENGTH, KEY_VALUE_HEADS, HEAD_WIDTH)
    prompt_value_rows = cached_prompt_values.astype(jnp.float32).reshape(PROMPT_LENGTH, KEY_VALUE_HEADS, HEAD_WIDTH)
    response_key_rows = rotated_response_keys.astype(jnp.float32).reshape(RESPONSE_ROWS, KEY_VALUE_HEADS, HEAD_WIDTH)
    response_value_rows = packed_response_values.astype(jnp.float32).reshape(RESPONSE_ROWS, KEY_VALUE_HEADS, HEAD_WIDTH)
    rows_per_block = math.gcd(RB, 64)
    block_count = RESPONSE_ROWS // rows_per_block
    column_ids = jnp.arange(RESPONSE_ROWS, dtype=jnp.int32)

    def one_block(block_index):
        first_row = (block_index * rows_per_block).astype(jnp.int32)
        query_head_count = lax.dynamic_slice_in_dim(queries, first_row, rows_per_block, 0)
        query_head_count = query_head_count.astype(jnp.float32).reshape(rows_per_block, KEY_VALUE_HEADS, group_width, HEAD_WIDTH)
        prompt_scores = jnp.einsum('rkgd,pkd->kgrp', query_head_count, prompt_key_rows) * score_scale
        resp_scores = jnp.einsum('rkgd,jkd->kgrj', query_head_count, response_key_rows) * score_scale
        row_ids = first_row + jnp.arange(rows_per_block, dtype=jnp.int32)
        own_segments = lax.dynamic_slice_in_dim(segment_ids, first_row, rows_per_block, 0)
        allowed = (segment_ids[None, :] == own_segments[:, None]) & (column_ids[None, :] <= row_ids[:, None])
        resp_scores = jnp.where(allowed, resp_scores, -1e+30)
        row_top = jnp.maximum(prompt_scores.max(axis=-1), resp_scores.max(axis=-1))
        prompt_exp = jnp.exp(prompt_scores - row_top[..., None])
        resp_exp = jnp.where(allowed, jnp.exp(resp_scores - row_top[..., None]), 0.0)
        row_total = prompt_exp.sum(axis=-1) + resp_exp.sum(axis=-1)
        prompt_probs = lax.optimization_barrier(prompt_exp.astype(jnp.bfloat16)).astype(jnp.float32)
        resp_probs = lax.optimization_barrier(resp_exp.astype(jnp.bfloat16)).astype(jnp.float32)
        numerator = jnp.einsum('kgrp,pkd->kgrd', prompt_probs, prompt_value_rows)
        numerator = numerator + jnp.einsum('kgrj,jkd->kgrd', resp_probs, response_value_rows)
        context = numerator / row_total[..., None]
        context = jnp.transpose(context, (2, 0, 1, 3)).reshape(rows_per_block, QUERY_HEADS * HEAD_WIDTH)
        return context.astype(jnp.bfloat16)
    context = lax.map(one_block, jnp.arange(block_count, dtype=jnp.int32)).reshape(RESPONSE_ROWS, QUERY_HEADS * HEAD_WIDTH)
    return jnp.dot(context, out_weight, preferred_element_type=jnp.float32).astype(jnp.bfloat16)
```

```python
import functools
import math

import jax
import jax.numpy as jnp
from jax import lax
from jax.experimental import pallas as pl
from jax.experimental.pallas import tpu as pltpu
from jax.sharding import PartitionSpec as P

WIDTH = 128
ROWS = 128
GROUP = 8
KEYS = 512
HALF = GROUP * ROWS
SCALE = math.log2(math.e) / math.sqrt(WIDTH)
MESH = pl.DeviceIdType.MESH
F32 = jnp.float32
BF16 = jnp.bfloat16
VMEM = pl.BlockSpec(memory_space=pltpu.VMEM)


def place():
    b, h = lax.axis_index("blk"), lax.axis_index("head")
    return b, h, b // 4, (b // 2) % 2, b % 2


def remote(src, dst, send, recv, device):
    return pltpu.make_async_remote_copy(
        src_ref=src, dst_ref=dst, send_sem=send, recv_sem=recv, device_id=device, device_id_type=MESH
    )


def with_ones(v):
    return jnp.concatenate([v, jnp.ones_like(v)], axis=1)


def dot_t(a, b):
    return lax.dot_general(a, b, (((1,), (1,)), ((), ())), preferred_element_type=F32)


def both(x):
    return jnp.concatenate([x, x], axis=1)


def attention(
    q_ref, k_ref, v_ref, rk_ref, rv_ref, seg_ref, w_ref,
    ctx_ref, wg_ref,
    q_other, qs, kb, vb, nk, nv, top, acc, part_out, part_in, lse_out, lse_in,
    ring_send, core_send, kv_recv, near_send, near_recv, q_sem, w_send, w_recv, part_send, part_recv,
):
    b, h, z, xh, c = place()
    up, down = ((b + 4) % 32, h), ((b + 28) % 32, h)
    across, mate = (b + 2 - 4 * xh, h), (b + 1 - 2 * c, h)
    after, before = ((b + 1) % 32, h), ((b + 31) % 32, h)
    g = xh * 2 + c
    g_across = 2 - 2 * xh + c
    g_mate = xh * 2 + 1 - c

    barrier = pltpu.get_barrier_semaphore()
    for device in (up, down, across, mate, after, before):
        pl.semaphore_signal(barrier, inc=1, device_id=device, device_id_type=MESH)
    kb[z, c] = k_ref[...]
    vb[z, c] = v_ref[...]
    wg_ref[g] = w_ref[...]
    pl.semaphore_wait(barrier, 6)

    buffers = (kb, vb)

    def ring(which, direction, slot):
        buf = buffers[which].at[slot, c]
        return remote(buf, buf, ring_send.at[which, direction, slot], kv_recv.at[which, slot, c], (up, down)[direction])

    def to_mate(which, slot):
        buf = buffers[which].at[slot, c]
        return remote(buf, buf, core_send.at[which, slot], kv_recv.at[which, slot, c], mate)

    def landed(which, slot, core):
        buf = buffers[which].at[slot, core]
        pltpu.make_async_copy(buf, buf, kv_recv.at[which, slot, core]).wait()

    send_q = remote(q_ref, q_other, q_sem.at[0], q_sem.at[1], across)
    send_nk = remote(rk_ref, nk, near_send.at[0], near_recv.at[0], after)
    send_nv = remote(rv_ref, nv, near_send.at[1], near_recv.at[1], after)
    w_across = remote(wg_ref.at[g], wg_ref.at[g], w_send.at[0], w_recv.at[0], across)
    w_mate = remote(wg_ref.at[g], wg_ref.at[g], w_send.at[1], w_recv.at[1], mate)
    w_on = remote(wg_ref.at[g_across], wg_ref.at[g_across], w_send.at[2], w_recv.at[2], mate)
    send_part = remote(part_out, part_in, part_send.at[0], part_recv.at[0], across)
    send_lse = remote(lse_out, lse_in, part_send.at[1], part_recv.at[1], across)

    for which in (0, 1):
        for direction in (0, 1):
            ring(which, direction, z).start()
    send_q.start()
    send_nk.start()
    send_nv.start()
    for which in (0, 1):
        to_mate(which, z).start()

    for n in range(GROUP):
        qs[pl.ds(n * ROWS, ROWS), :] = q_ref[:, n * WIDTH : (n + 1) * WIDTH]
    other = pl.ds(HALF, HALF)
    top[other, :] = jnp.full((HALF, WIDTH), -1e30, F32)
    acc[other, :] = jnp.zeros((HALF, 2 * WIDTH), F32)

    own_ids = seg_ref[pl.ds(b, 1), :].astype(F32)
    before_ids = seg_ref[pl.ds(jnp.maximum(b - 1, 0), 1), :].astype(F32)
    row_ids = jnp.transpose(jnp.broadcast_to(own_ids, (ROWS, ROWS)))
    row = lax.broadcasted_iota(jnp.int32, (ROWS, ROWS), 0)
    column = lax.broadcasted_iota(jnp.int32, (ROWS, ROWS), 1)
    allow_own = (row_ids == jnp.broadcast_to(own_ids, (ROWS, ROWS))) & (column <= row)
    first = jnp.broadcast_to(b, (ROWS, ROWS)) > 0
    allow_before = (row_ids == jnp.broadcast_to(before_ids, (ROWS, ROWS))) & first
    bias = jnp.concatenate([jnp.where(allow_before, 1.0, 0.0), jnp.where(allow_own, 1.0, 0.0)], axis=1)
    allowed = bias > 0.5
    send_nk.wait_recv()
    send_nv.wait_recv()
    near_k = jnp.concatenate([nk[...], rk_ref[...]], axis=0)
    near_v = with_ones(jnp.concatenate([nv[...], rv_ref[...]], axis=0))
    for n in range(GROUP):
        rows = pl.ds(n * ROWS, ROWS)
        s = jnp.where(allowed, dot_t(qs[rows, :], near_k), -1e30)
        m = jnp.max(s, axis=1, keepdims=True) * SCALE
        p = jnp.where(allowed, jnp.exp2(s * SCALE - m), 0.0)
        acc[rows, :] = jnp.dot(p.astype(BF16), near_v, preferred_element_type=F32)
        top[rows, :] = jnp.broadcast_to(m, (ROWS, WIDTH))

    def tile(rows, keys, values):
        s = dot_t(qs[rows, :], keys)
        old = top[rows, :]
        new = jnp.maximum(old, jnp.max(s, axis=1, keepdims=True) * SCALE)
        shrink = jnp.exp2(old - new)
        p = jnp.exp2(s * SCALE - new[:, :1]).astype(BF16)
        acc[rows, :] = acc[rows, :] * both(shrink) + jnp.dot(p, values, preferred_element_type=F32)
        top[rows, :] = new

    def arrived(u):
        a, odd = (u + 1) // 2, u % 2
        slot = (z + a * (1 - 2 * odd) + 8) % 8
        landed(0, slot, c)
        landed(1, slot, c)
        to_mate(0, slot).start()
        to_mate(1, slot).start()

        @pl.when((odd == 1) & (a <= 3))
        def _():
            ring(0, 0, slot).start()

        @pl.when((odd == 1) & (a <= 2))
        def _():
            ring(1, 0, slot).start()

        @pl.when((odd == 0) & (a <= 2))
        def _():
            ring(0, 1, slot).start()

        @pl.when((odd == 0) & (a <= 3))
        def _():
            ring(1, 1, slot).start()

    eye = row == column

    def step(t, _):
        a, odd = (t + 1) // 2, t % 2
        slot = (z + a * (1 - 2 * odd) + 8) % 8
        landed(0, slot, 1 - c)
        landed(1, slot, 1 - c)

        def half(i, _):
            side = jnp.where(t == 0, i, 1 - i)

            @pl.when((t == 0) & (i == 1))
            def _():
                send_q.wait_recv()
                for n in range(GROUP):
                    qs[pl.ds(HALF + n * ROWS, ROWS), :] = q_other[:, n * WIDTH : (n + 1) * WIDTH]

            keys = kb[slot].reshape(2 * KEYS, WIDTH)
            values = with_ones(vb[slot].reshape(2 * KEYS, WIDTH))
            for n in range(GROUP):
                tile(pl.ds(pl.multiple_of(side * HALF + n * ROWS, ROWS), ROWS), keys, values)

            @pl.when((t == 7) & (i == 0))
            def _():
                for n in range(GROUP):
                    rows = pl.ds(HALF + n * ROWS, ROWS)
                    total = acc[rows, WIDTH:]
                    part_out[:, n * WIDTH : (n + 1) * WIDTH] = (acc[rows, :WIDTH] / total).astype(BF16)
                    lse = top[rows, :] + jnp.log2(total)
                    lse_out[pl.ds(n, 1), :] = jnp.sum(jnp.where(eye, lse, 0.0), axis=0, keepdims=True)
                send_part.start()
                send_lse.start()

            return 0

        lax.fori_loop(0, 2, half, 0)

        @pl.when((odd == 0) & (t < 6))
        def _():
            arrived(t + 1)
            arrived(t + 2)

        @pl.when(t == 6)
        def _():
            arrived(t + 1)
            w_across.wait_recv()
            w_on.start()

        @pl.when(t == 1)
        def _():
            w_across.start()
            w_mate.start()

        return 0

    lax.fori_loop(0, 8, step, 0)

    send_lse.wait_recv()
    send_part.wait_recv()
    for n in range(GROUP):
        rows = pl.ds(n * ROWS, ROWS)
        columns = slice(n * WIDTH, (n + 1) * WIDTH)
        total = acc[rows, WIDTH:]
        here = top[rows, :] + jnp.log2(total)
        there = jnp.transpose(jnp.broadcast_to(lse_in[pl.ds(n, 1), :], (ROWS, ROWS)))
        high = jnp.maximum(here, there)
        a, d = jnp.exp2(here - high), jnp.exp2(there - high)
        mixed = acc[rows, :WIDTH] * (a / total) + part_in[:, columns].astype(F32) * d
        ctx_ref[:, columns] = (mixed / (a + d)).astype(BF16)

    for which in (0, 1):
        ring(which, 0, z).wait_send()
        ring(which, 1, z).wait_send()
        for a in (1, 2, 3):
            if a <= 3 - which:
                ring(which, 0, (z + 8 - a) % 8).wait_send()
            if a <= 2 + which:
                ring(which, 1, (z + a) % 8).wait_send()
        for slot in range(8):
            to_mate(which, slot).wait_send()
    send_q.wait_send()
    send_nk.wait_send()
    send_nv.wait_send()
    send_part.wait_send()
    send_lse.wait_send()
    w_mate.wait()
    w_across.wait_send()
    w_on.wait()


def attend(q, k, v, rk, rv, seg, w):
    dma = pltpu.SemaphoreType.DMA
    return pl.pallas_call(
        attention,
        out_shape=(
            jax.ShapeDtypeStruct((ROWS, HALF), BF16),
            jax.ShapeDtypeStruct((4, 1024, 256), BF16),
        ),
        in_specs=[VMEM] * 7,
        out_specs=(VMEM, VMEM),
        scratch_shapes=[
            pltpu.VMEM((ROWS, HALF), BF16),
            pltpu.VMEM((2 * HALF, WIDTH), BF16),
            pltpu.VMEM((8, 2, KEYS, WIDTH), BF16),
            pltpu.VMEM((8, 2, KEYS, WIDTH), BF16),
            pltpu.VMEM((ROWS, WIDTH), BF16),
            pltpu.VMEM((ROWS, WIDTH), BF16),
            pltpu.VMEM((2 * HALF, WIDTH), F32),
            pltpu.VMEM((2 * HALF, 2 * WIDTH), F32),
            pltpu.VMEM((ROWS, HALF), BF16),
            pltpu.VMEM((ROWS, HALF), BF16),
            pltpu.VMEM((GROUP, ROWS), F32),
            pltpu.VMEM((GROUP, ROWS), F32),
            dma((2, 2, 8)),
            dma((2, 8)),
            dma((2, 8, 2)),
            dma((2,)),
            dma((2,)),
            dma((2,)),
            dma((3,)),
            dma((3,)),
            dma((2,)),
            dma((2,)),
        ],
        compiler_params=pltpu.CompilerParams(
            collective_id=0, has_side_effects=True, vmem_limit_bytes=48 * 2**20
        ),
    )(q, k, v, rk, rv, seg, w)


SUB = ROWS // 8


def projection(
    ctx_ref, w_ref, out_ref,
    cb, ps, pr, red, zr,
    ring_send, ring_recv, ps_send, ps_recv, z_send, z_recv, h_send, h_recv,
):
    b, h, z, xh, c = place()
    up, down = ((b + 4) % 32, h), ((b + 28) % 32, h)

    def at_z(n):
        return ((b + 4 * n) % 32, h)

    def at_h(n):
        return (b, (h + n) % 8)

    barrier = pltpu.get_barrier_semaphore()
    for n in range(1, 8):
        pl.semaphore_signal(barrier, inc=1, device_id=at_z(n), device_id_type=MESH)
        pl.semaphore_signal(barrier, inc=1, device_id=at_h(n), device_id_type=MESH)
    cb[z] = ctx_ref[...]
    pl.semaphore_wait(barrier, 14)

    def ring(part, direction, slot):
        buf = cb.at[slot, :, pl.ds(part * 512, 512)]
        return remote(buf, buf, ring_send.at[part, direction, slot], ring_recv.at[part, slot], (up, down)[direction])

    def landed(part, slot):
        buf = cb.at[slot, :, pl.ds(part * 512, 512)]
        pltpu.make_async_copy(buf, buf, ring_recv.at[part, slot]).wait()

    for part in (0, 1):
        for direction in (0, 1):
            ring(part, direction, z).start()

    def sub(n):
        return pl.ds(pl.multiple_of(n * SUB, SUB), SUB)

    def partial_to(slot, n):
        there = (h + n) % 8
        return remote(
            ps.at[slot, sub(there)], pr.at[slot, h], ps_send.at[slot, there], ps_recv.at[slot, h], (b, there)
        )

    def slot_of(t):
        a, odd = (t + 1) // 2, t % 2
        return (z + a * (1 - 2 * odd) + 8) % 8

    def arrived(u):
        a, odd = (u + 1) // 2, u % 2
        slot = slot_of(u)
        landed(0, slot)
        landed(1, slot)

        @pl.when((odd == 1) & (a <= 3))
        def _():
            ring(0, 0, slot).start()

        @pl.when((odd == 1) & (a <= 2))
        def _():
            ring(1, 0, slot).start()

        @pl.when((odd == 0) & (a <= 2))
        def _():
            ring(0, 1, slot).start()

        @pl.when((odd == 0) & (a <= 3))
        def _():
            ring(1, 1, slot).start()

    def step(t, _):
        slot = slot_of(t)

        @pl.when((t % 2 == 1) & (t < 7))
        def _():
            arrived(t)
            arrived(t + 1)

        @pl.when(t == 7)
        def _():
            arrived(t)

        rows = cb[slot]
        for part in range(4):
            ps[slot, :, part * 256 : (part + 1) * 256] = jnp.dot(
                rows, w_ref[part], preferred_element_type=F32
            ).astype(BF16)
        for n in range(1, 8):
            partial_to(slot, n).start()
        pr[slot, h] = ps[slot, sub(h), :]
        return 0

    lax.fori_loop(0, 8, step, 0)

    def to_z(slot):
        return remote(red.at[slot], zr.at[z], z_send.at[slot], z_recv.at[z], (slot * 4 + xh * 2 + c, h))

    def total(t, _):
        slot = slot_of(t)
        for n in range(1, 8):
            there = (h + n) % 8
            buf = pr.at[slot, there]
            pltpu.make_async_copy(buf, buf, ps_recv.at[slot, there]).wait()
        value = pr[slot, 0].astype(F32)
        for n in range(1, 8):
            value = value + pr[slot, n].astype(F32)
        red[slot] = value.astype(BF16)

        @pl.when(t == 0)
        def _():
            zr[z] = red[z]

        @pl.when(t > 0)
        def _():
            to_z(slot).start()

        return 0

    lax.fori_loop(0, 8, total, 0)

    def to_h(there):
        return remote(zr.at[there], out_ref.at[sub(h)], h_send.at[there], h_recv.at[h], (b, there))

    def last(t, _):
        slot = slot_of(t)

        @pl.when(t > 0)
        def _():
            buf = zr.at[slot]
            pltpu.make_async_copy(buf, buf, z_recv.at[slot]).wait()

        @pl.when(slot != h)
        def _():
            to_h(slot).start()

        @pl.when(slot == h)
        def _():
            out_ref[sub(h), :] = zr[h]

        return 0

    lax.fori_loop(0, 8, last, 0)

    for n in range(1, 8):
        there = (h + n) % 8
        buf = out_ref.at[sub(there)]
        pltpu.make_async_copy(buf, buf, h_recv.at[there]).wait()
    for n in range(1, 8):
        to_h((h + n) % 8).wait_send()
        to_z((z + n) % 8).wait_send()

    def sent(slot, _):
        for n in range(1, 8):
            partial_to(slot, n).wait_send()
        return 0

    lax.fori_loop(0, 8, sent, 0)
    for part in (0, 1):
        ring(part, 0, z).wait_send()
        ring(part, 1, z).wait_send()
        for a in (1, 2, 3):
            if a <= 3 - part:
                ring(part, 0, (z + 8 - a) % 8).wait_send()
            if a <= 2 + part:
                ring(part, 1, (z + a) % 8).wait_send()


def project(ctx, w):
    dma = pltpu.SemaphoreType.DMA
    return pl.pallas_call(
        projection,
        out_shape=jax.ShapeDtypeStruct((ROWS, 1024), BF16),
        in_specs=[VMEM] * 2,
        out_specs=VMEM,
        scratch_shapes=[
            pltpu.VMEM((8, ROWS, 1024), BF16),
            pltpu.VMEM((8, ROWS, 1024), BF16),
            pltpu.VMEM((8, 8, SUB, 1024), BF16),
            pltpu.VMEM((8, SUB, 1024), BF16),
            pltpu.VMEM((8, SUB, 1024), BF16),
            dma((2, 2, 8)),
            dma((2, 8)),
            dma((8, 8)),
            dma((8, 8)),
            dma((8,)),
            dma((8,)),
            dma((8,)),
            dma((8,)),
        ],
        compiler_params=pltpu.CompilerParams(
            collective_id=1, has_side_effects=True, vmem_limit_bytes=48 * 2**20
        ),
    )(ctx, w)


def on_device(q, k, v, rk, rv, seg, w):
    ctx, gathered = attend(q, k, v, rk, rv, seg.reshape(32, ROWS), w)
    return project(ctx, gathered)


def solution(mesh):
    return jax.shard_map(
        on_device,
        mesh=mesh,
        in_specs=(
            P("blk", "head"),
            P("blk", "head"),
            P("blk", "head"),
            P("blk", "head"),
            P("blk", "head"),
            P(),
            P("head", "blk"),
        ),
        out_specs=P("blk", "head"),
        check_vma=False,
    )
```

```python
import functools
import math

import jax
import jax.numpy as jnp
from jax import lax
from jax.experimental import pallas as pl
from jax.experimental.pallas import tpu as pltpu
from jax.sharding import PartitionSpec as P

WIDTH = 128
ROWS = 128
GROUP = 8
PIECE = 256
SIDE = ROWS // 2
HALF = GROUP * ROWS
SCALE = math.log2(math.e) / math.sqrt(WIDTH)
MESH = pl.DeviceIdType.MESH
F32 = jnp.float32
BF16 = jnp.bfloat16
VMEM = pl.BlockSpec(memory_space=pltpu.VMEM)
ANY = pl.BlockSpec(memory_space=pl.ANY)


def place():
    b, h = lax.axis_index("blk"), lax.axis_index("head")
    return b, h, b // 4, (b // 2) % 2, b % 2


def remote(src, dst, send, recv, device):
    return pltpu.make_async_remote_copy(
        src_ref=src, dst_ref=dst, send_sem=send, recv_sem=recv, device_id=device, device_id_type=MESH
    )


def with_ones(v):
    return jnp.concatenate([v, jnp.ones_like(v)], axis=1)


def dot_t(a, b):
    return lax.dot_general(a, b, (((1,), (1,)), ((), ())), preferred_element_type=F32)


def both(x):
    return jnp.concatenate([x, x], axis=1)


def local(src, dst, sem):
    return pltpu.make_async_copy(src, dst, sem)


def waited(buf, sem):
    pltpu.make_async_copy(buf, buf, sem).wait()


def whole(
    q_hbm, k_hbm, v_hbm, rk_hbm, rv_hbm, seg_hbm, w_hbm,
    out_ref,
    q_ref, q_other, qs, qs_x, kv, near, seg_ref, top, top_x, acc, acc_x, part_out, part_in, lse_out, lse_in,
    wg, cb, half_sum, ps, pr, red, zr,
    load, ring_send, ring_recv, core_send, core_recv, near_send, near_recv, q_sem, w_send, w_recv,
    part_send, part_recv, lse_send, lse_recv, cb_send, cb_recv, ps_send, ps_recv, z_send, z_recv, h_send, h_recv,
):
    b, h, z, xh, c = place()
    up, down = ((b + 4) % 32, h), ((b + 28) % 32, h)
    across, mate = (b + 2 - 4 * xh, h), (b + 1 - 2 * c, h)
    after, before = ((b + 1) % 32, h), ((b + 31) % 32, h)
    g = xh * 2 + c
    y, xl = h // 2, h % 2
    beside, diagonal = (b, h + 1 - 2 * xl), (b + 2 - 4 * xh, h + 1 - 2 * xl)

    loads = [
        local(k_hbm.at[pl.ds(0, PIECE)], kv.at[0, 0, c, 0], load.at[0]),
        local(v_hbm.at[pl.ds(0, PIECE)], kv.at[0, 0, c, 1], load.at[1]),
        local(k_hbm.at[pl.ds(PIECE, PIECE)], kv.at[0, 1, c, 0], load.at[2]),
        local(v_hbm.at[pl.ds(PIECE, PIECE)], kv.at[0, 1, c, 1], load.at[3]),
        local(q_hbm, q_ref, load.at[4]),
        local(rk_hbm, near.at[0, 1], load.at[5]),
        local(rv_hbm, near.at[1, 1], load.at[6]),
        local(seg_hbm, seg_ref, load.at[7]),
        local(w_hbm, wg.at[0, g], load.at[8]),
    ]
    for copy in loads:
        copy.start()

    barrier = pltpu.get_barrier_semaphore()
    partners = [across, diagonal, mate, after, before]
    partners += [((b + 4 * n) % 32, h) for n in range(1, 8)] + [(b, (h + n) % 8) for n in range(1, 8)]
    for device in partners:
        pl.semaphore_signal(barrier, inc=1, device_id=device, device_id_type=MESH)
    pl.semaphore_wait(barrier, len(partners))

    def ring(buf, send, recv, u, d):
        def go(src):
            return remote(src, buf(u, d), send.at[u, d], recv.at[u, d], (up, down)[d])

        return go

    def kv_at(u, d):
        return kv.at[u, d, c]

    def cb_at(u, d):
        return cb.at[u, d]

    def pass_on(at, send, recv, u):
        for d in (0, 1):
            waited(at(u, d), recv.at[u, d])

            @pl.when(u <= 4)
            def _():
                ring(at, send, recv, u + 2, d)(at(u, d)).start()

            @pl.when(u == 5 + d)
            def _():
                ring(at, send, recv, 7, d)(at(u, d)).start()

    def begin(at, send, recv, piece):
        for d in (0, 1):
            ring(at, send, recv, 1 + piece, d)(at(0, piece)).start()

    def all_sent(at, send, recv):
        for u in range(1, 8):
            for d in (0, 1):
                ring(at, send, recv, u, d)(at(u, d)).wait_send()

    def to_mate(u, d):
        return remote(kv_at(u, d), kv_at(u, d), core_send.at[u, d], core_recv.at[u, d], mate)

    send_q = remote(q_hbm, q_other, q_sem.at[0], q_sem.at[1], across)
    send_nk = remote(rk_hbm, near.at[0, 0], near_send.at[0], near_recv.at[0], after)
    send_nv = remote(rv_hbm, near.at[1, 0], near_send.at[1], near_recv.at[1], after)
    def spread_w(k):
        source, dest = wg.at[0, g], wg.at[(0, 1, 1)[k], g]
        return remote(source, dest, w_send.at[k], w_recv.at[k], (across, diagonal, beside)[k])

    g_across = 2 - 2 * xh + c

    def mate_w(k):
        buf = wg.at[(0, 1, 1, 0)[k], (g_across, g_across, g, g)[k]]
        return remote(buf, buf, w_send.at[3 + k], w_recv.at[3 + k], mate)

    def send_part(part):
        return remote(
            part_out.at[part], part_in.at[part], part_send.at[part], part_recv.at[part], (across, diagonal, beside)[part]
        )

    def send_lse(part):
        return remote(
            lse_out.at[part], lse_in.at[part], lse_send.at[part], lse_recv.at[part], (across, diagonal, beside)[part]
        )

    send_q.start()
    send_nk.start()
    send_nv.start()
    loads[0].wait()
    loads[1].wait()
    begin(kv_at, ring_send, ring_recv, 0)
    loads[2].wait()
    loads[3].wait()
    begin(kv_at, ring_send, ring_recv, 1)
    to_mate(0, 0).start()
    to_mate(0, 1).start()
    for copy in loads[4:]:
        copy.wait()

    for n in range(GROUP):
        for p in (0, 1):
            qs[pl.ds(p * 512 + n * SIDE, SIDE), :] = q_ref[p * SIDE : (p + 1) * SIDE, n * WIDTH : (n + 1) * WIDTH]
    top_x[...] = jnp.full((HALF, WIDTH), -1e30, F32)
    acc_x[...] = jnp.zeros((HALF, 2 * WIDTH), F32)

    own_ids = seg_ref[pl.ds(b, 1), :].astype(F32)
    before_ids = seg_ref[pl.ds(jnp.maximum(b - 1, 0), 1), :].astype(F32)
    row_ids = jnp.transpose(jnp.broadcast_to(own_ids, (ROWS, ROWS)))
    row = lax.broadcasted_iota(jnp.int32, (ROWS, ROWS), 0)
    column = lax.broadcasted_iota(jnp.int32, (ROWS, ROWS), 1)
    allow_own = (row_ids == jnp.broadcast_to(own_ids, (ROWS, ROWS))) & (column <= row)
    first = jnp.broadcast_to(b, (ROWS, ROWS)) > 0
    allow_before = (row_ids == jnp.broadcast_to(before_ids, (ROWS, ROWS))) & first
    allowed = jnp.concatenate([jnp.where(allow_before, 1.0, 0.0), jnp.where(allow_own, 1.0, 0.0)], axis=1)
    allowed = [jnp.concatenate([allowed[p * SIDE : (p + 1) * SIDE]] * 2, axis=0) > 0.5 for p in (0, 1)]
    send_nk.wait_recv()
    send_nv.wait_recv()
    near_k = near[0].reshape(2 * ROWS, WIDTH)
    near_v = with_ones(near[1].reshape(2 * ROWS, WIDTH))
    for n in range(GROUP):
        rows = pl.ds(n * ROWS, ROWS)
        s = jnp.where(allowed[n // 4], dot_t(qs[rows, :], near_k), -1e30)
        m = jnp.max(s, axis=1, keepdims=True) * SCALE
        p = jnp.where(allowed[n // 4], jnp.exp2(s * SCALE - m), 0.0)
        acc[rows, :] = jnp.dot(p.astype(BF16), near_v, preferred_element_type=F32)
        top[rows, :] = jnp.broadcast_to(m, (ROWS, WIDTH))

    own, partner = (qs, top, acc), (qs_x, top_x, acc_x)

    def tile(refs, n, keys, values):
        q, t, total = refs
        rows = pl.ds(n, ROWS) if isinstance(n, int) else pl.ds(pl.multiple_of(n, ROWS), ROWS)
        s = dot_t(q[rows, :], keys)
        old = t[rows, :]
        new = jnp.maximum(old, jnp.max(s, axis=1, keepdims=True) * SCALE)
        shrink = jnp.exp2(old - new)
        p = jnp.exp2(s * SCALE - new[:, :1]).astype(BF16)
        total[rows, :] = total[rows, :] * both(shrink) + jnp.dot(p, values, preferred_element_type=F32)
        t[rows, :] = new

    eye = row == column

    def unit(u):
        keys = kv[u, :, :, 0].reshape(4 * PIECE, WIDTH)
        return keys, with_ones(kv[u, :, :, 1].reshape(4 * PIECE, WIDTH))

    def step(t, _):
        new = (t <= 1) | ((t >= 4) & (t <= 8)) | (t == 10)
        u = jnp.where(t <= 1, t, jnp.where(t <= 3, t - 2, jnp.where(t <= 8, t - 2, jnp.where(t == 9, 6, 7))))

        @pl.when(new)
        def _():
            for d in (0, 1):
                waited(kv.at[u, d, 1 - c], core_recv.at[u, d])

        @pl.when(t == 2)
        def _():
            send_q.wait_recv()
            for n in range(GROUP):
                for p in (0, 1):
                    x = q_other[p * SIDE : (p + 1) * SIDE, n * WIDTH : (n + 1) * WIDTH]
                    qs_x[pl.ds(p * 512 + n * SIDE, SIDE), :] = x

        @pl.when((t <= 1) | (t == 9))
        def _():
            keys, values = unit(u)
            for n in range(GROUP):
                tile(own, n * ROWS, keys, values)

        @pl.when((t == 2) | (t == 3) | (t == 8))
        def _():
            keys, values = unit(u)
            for n in range(GROUP):
                tile(partner, n * ROWS, keys, values)

        @pl.when((t >= 4) & (t <= 7))
        def _():
            keys, values = unit(u)
            for n in range(GROUP):
                tile(partner, n * ROWS, keys, values)
                tile(own, n * ROWS, keys, values)

        @pl.when(t == 10)
        def _():
            keys, values = unit(u)
            for part in (0, 1, 2):
                refs = (partner, partner, own)[part]
                base = xl * 512 if part == 0 else (1 - xl) * 512
                for n in range(4):
                    tile(refs, base + n * ROWS, keys, values)
                for n in range(4):
                    rows = pl.ds(pl.multiple_of(base + n * ROWS, ROWS), ROWS)
                    total = refs[2][rows, WIDTH:]
                    part_out[part, pl.ds(n * ROWS, ROWS), :] = (refs[2][rows, :WIDTH] / total).astype(BF16)
                    lse = refs[1][rows, :] + jnp.log2(total)
                    lse_out[part, pl.ds(n, 1), :] = jnp.sum(jnp.where(eye, lse, 0.0), axis=0, keepdims=True)
                send_part(part).start()
                send_lse(part).start()
            for n in range(4):
                tile(own, xl * 512 + n * ROWS, keys, values)

        @pl.when((t <= 1) | ((t >= 3) & (t <= 6)) | (t == 8))
        def _():
            after_it = jnp.where(t <= 1, t + 1, jnp.where(t == 8, 7, t))
            pass_on(kv_at, ring_send, ring_recv, after_it)
            to_mate(after_it, 0).start()
            to_mate(after_it, 1).start()

        @pl.when(t == 0)
        def _():
            for k in (2, 1, 0):
                spread_w(k).start()
            mate_w(3).start()

        @pl.when(t == 6)
        def _():
            for k in (1, 2):
                spread_w(k).wait_recv()
                mate_w(k).start()

        @pl.when(t == 9)
        def _():
            spread_w(0).wait_recv()
            mate_w(0).start()

        return 0

    lax.fori_loop(0, 11, step, 0)

    def column(part, n):
        return jnp.transpose(jnp.broadcast_to(lse_in[part, pl.ds(n, 1), :], (ROWS, ROWS)))

    def mix(piece, n, o, lse, part):
        there = column(part, n)
        high = jnp.maximum(lse, there)
        a, d = jnp.exp2(lse - high), jnp.exp2(there - high)
        mixed = o * a + part_in[part, pl.ds(n * ROWS, ROWS), :].astype(F32) * d
        mixed = (mixed / (a + d)).astype(BF16)
        cb[0, piece, :, 2 * n * WIDTH : (2 * n + 1) * WIDTH] = mixed[:SIDE]
        cb[0, piece, :, (2 * n + 1) * WIDTH : (2 * n + 2) * WIDTH] = mixed[SIDE:]

    def received(part):
        send_part(part).wait_recv()
        send_lse(part).wait_recv()

    received(0)
    for n in range(4):
        rows = pl.ds(pl.multiple_of(xl * 512 + n * ROWS, ROWS), ROWS)
        total = acc[rows, WIDTH:]
        mix(0, n, acc[rows, :WIDTH] / total, top[rows, :] + jnp.log2(total), 0)
    begin(cb_at, cb_send, cb_recv, 0)
    received(1)
    received(2)
    for n in range(4):
        mix(1, n, part_in[1, pl.ds(n * ROWS, ROWS), :].astype(F32), column(1, n), 2)
    begin(cb_at, cb_send, cb_recv, 1)

    for k in range(4):
        mate_w(k).wait_recv()

    def partial_to(k, there):
        return remote(ps.at[k, there], pr.at[k, y], ps_send.at[k, there], ps_recv.at[k, y], (b, there * 2 + xl))

    def each_y(act):
        for n in range(1, 4):
            act((y + n) % 4)

    def spread(k):
        each_y(lambda there: partial_to(k, there).start())

    def alone(k, u):
        for q in range(4):
            value = jnp.dot(cb[u, 0], wg[0, q], preferred_element_type=F32)
            value = value + jnp.dot(cb[u, 1], wg[1, q], preferred_element_type=F32)
            ps[k, q, 0] = value.astype(BF16)
            ps[k, q, 1] = jnp.zeros((SIDE, 256), BF16)
        spread(k)

    def to_z(k, d):
        there = (z + k * (2 * d - 1) + 8) % 8
        return remote(red.at[k, d], zr.at[z], z_send.at[k, d], z_recv.at[z], (there * 4 + g, h))

    def sum_up(k):
        each_y(lambda there: waited(pr.at[k, there], ps_recv.at[k, there]))
        value = ps[k, y].astype(F32)
        for n in range(1, 4):
            value = value + pr[k, (y + n) % 4].astype(F32)
        red[k] = value.astype(BF16)

        @pl.when(k > 0)
        def _():
            to_z(k, 0).start()

        @pl.when((k > 0) & (k < 4))
        def _():
            to_z(k, 1).start()

    def out_at(row_half, block):
        rows = pl.ds(pl.multiple_of(row_half * SIDE, SIDE), SIDE)
        return out_ref.at[rows, pl.ds(pl.multiple_of(block * 256, 256), 256)]

    def to_h(buf, there):
        return remote(buf, out_at(xl, y), h_send.at[there], h_recv.at[h], (b, there))

    def hand_over(buf, source):
        @pl.when(source != h)
        def _():
            to_h(buf, source).start()

        @pl.when(source == h)
        def _():
            out_at(xl, y)[...] = buf[...]

    def deliver(k, d):
        source = (z + k * (1 - 2 * d) + 8) % 8
        waited(zr.at[source], z_recv.at[source])
        hand_over(zr.at[source], source)

    alone(0, 0)

    def stage(k, _):
        u = 2 * k - 1
        pass_on(cb_at, cb_send, cb_recv, u)
        rows = cb[u].reshape(ROWS, 1024)
        for q in range(4):
            half_sum[q] = jnp.dot(rows, wg[0, q], preferred_element_type=F32)
        pass_on(cb_at, cb_send, cb_recv, u + 1)
        rows = cb[u + 1].reshape(ROWS, 1024)
        for q in range(4):
            value = (half_sum[q] + jnp.dot(rows, wg[1, q], preferred_element_type=F32)).astype(BF16)
            ps[k, q] = value.reshape(2, SIDE, 256)
        spread(k)

        @pl.when(k >= 2)
        def _():
            sum_up(k - 1)

        @pl.when(k == 3)
        def _():
            deliver(1, 0)
            deliver(1, 1)

        return 0

    lax.fori_loop(1, 4, stage, 0)
    sum_up(0)
    hand_over(red.at[0, 0], z)
    pass_on(cb_at, cb_send, cb_recv, 7)
    alone(4, 7)
    sum_up(3)
    deliver(2, 0)
    deliver(2, 1)
    sum_up(4)
    deliver(3, 0)
    deliver(3, 1)
    deliver(4, 0)

    for n in range(1, 8):
        source = (h + n) % 8
        waited(out_at(source % 2, source // 2), h_recv.at[source])

    for n in range(8):
        source = (z + n) % 8

        @pl.when(source != h)
        def _():
            to_h(zr.at[source], source).wait_send()

    for k in range(5):
        each_y(lambda there: partial_to(k, there).wait_send())
        if k > 0:
            to_z(k, 0).wait_send()
        if 0 < k < 4:
            to_z(k, 1).wait_send()
    all_sent(cb_at, cb_send, cb_recv)
    all_sent(kv_at, ring_send, ring_recv)
    for u in range(8):
        for d in (0, 1):
            to_mate(u, d).wait_send()
    send_q.wait_send()
    send_nk.wait_send()
    send_nv.wait_send()
    for k in range(3):
        send_part(k).wait_send()
        send_lse(k).wait_send()
        spread_w(k).wait_send()
    for k in range(4):
        mate_w(k).wait_send()


def on_device(q, k, v, rk, rv, seg, w):
    dma = pltpu.SemaphoreType.DMA
    return pl.pallas_call(
        whole,
        out_shape=jax.ShapeDtypeStruct((ROWS, 1024), BF16),
        in_specs=[ANY] * 7,
        out_specs=VMEM,
        scratch_shapes=[
            pltpu.VMEM((ROWS, HALF), BF16),
            pltpu.VMEM((ROWS, HALF), BF16),
            pltpu.VMEM((HALF, WIDTH), BF16),
            pltpu.VMEM((HALF, WIDTH), BF16),
            pltpu.VMEM((8, 2, 2, 2, PIECE, WIDTH), BF16),
            pltpu.VMEM((2, 2, ROWS, WIDTH), BF16),
            pltpu.VMEM((32, ROWS), jnp.int32),
            pltpu.VMEM((HALF, WIDTH), F32),
            pltpu.VMEM((HALF, WIDTH), F32),
            pltpu.VMEM((HALF, 2 * WIDTH), F32),
            pltpu.VMEM((HALF, 2 * WIDTH), F32),
            pltpu.VMEM((3, 4 * ROWS, WIDTH), BF16),
            pltpu.VMEM((3, 4 * ROWS, WIDTH), BF16),
            pltpu.VMEM((3, 4, ROWS), F32),
            pltpu.VMEM((3, 4, ROWS), F32),
            pltpu.VMEM((2, 4, 1024, 256), BF16),
            pltpu.VMEM((8, 2, SIDE, 1024), BF16),
            pltpu.VMEM((4, ROWS, 256), F32),
            pltpu.VMEM((5, 4, 2, SIDE, 256), BF16),
            pltpu.VMEM((5, 4, 2, SIDE, 256), BF16),
            pltpu.VMEM((5, 2, SIDE, 256), BF16),
            pltpu.VMEM((8, SIDE, 256), BF16),
            dma((9,)),
            dma((8, 2)), dma((8, 2)),
            dma((8, 2)), dma((8, 2)),
            dma((2,)), dma((2,)),
            dma((2,)),
            dma((7,)), dma((7,)),
            dma((3,)), dma((3,)),
            dma((3,)), dma((3,)),
            dma((8, 2)), dma((8, 2)),
            dma((5, 4)), dma((5, 4)),
            dma((5, 2)), dma((8,)),
            dma((8,)), dma((8,)),
        ],
        compiler_params=pltpu.CompilerParams(
            collective_id=0, has_side_effects=True, vmem_limit_bytes=56 * 2**20
        ),
    )(q, k, v, rk, rv, seg.reshape(32, ROWS), w)


def solution(mesh):
    return jax.shard_map(
        on_device,
        mesh=mesh,
        in_specs=(
            P("blk", "head"),
            P("blk", "head"),
            P("blk", "head"),
            P("blk", "head"),
            P("blk", "head"),
            P(),
            P("head", "blk"),
        ),
        out_specs=P("blk", "head"),
        check_vma=False,
    )
```

```python
import functools
import math

import jax
import jax.numpy as jnp
from jax import lax
from jax.experimental import pallas as pl
from jax.experimental.pallas import tpu as pltpu
from jax.sharding import PartitionSpec as P

WIDTH = 128
ROWS = 128
GROUP = 8
PIECE = 256
SIDE = ROWS // 2
HALF = GROUP * ROWS
SCALE = math.log2(math.e) / math.sqrt(WIDTH)
MESH = pl.DeviceIdType.MESH
F32 = jnp.float32
BF16 = jnp.bfloat16
VMEM = pl.BlockSpec(memory_space=pltpu.VMEM)
ANY = pl.BlockSpec(memory_space=pl.ANY)


def place():
    b, h = lax.axis_index("blk"), lax.axis_index("head")
    return b, h, b // 4, (b // 2) % 2, b % 2


def remote(src, dst, send, recv, device):
    return pltpu.make_async_remote_copy(
        src_ref=src, dst_ref=dst, send_sem=send, recv_sem=recv, device_id=device, device_id_type=MESH
    )


def with_ones(v):
    return jnp.concatenate([v, jnp.ones_like(v)], axis=1)


def dot_t(a, b):
    return lax.dot_general(a, b, (((1,), (1,)), ((), ())), preferred_element_type=F32)


def both(x):
    return jnp.concatenate([x, x], axis=1)


def local(src, dst, sem):
    return pltpu.make_async_copy(src, dst, sem)


def waited(buf, sem):
    pltpu.make_async_copy(buf, buf, sem).wait()


def whole(
    q_hbm, k_hbm, v_hbm, rk_hbm, rv_hbm, seg_hbm, w_hbm,
    out_ref,
    q_ref, q_other, qs, qs_x, kv, near, seg_ref, top, top_x, acc, acc_x, part_out, part_in, lse_out, lse_in,
    wg, cb, half_sum, ps, pr, red, zr,
    load, ring_send, ring_recv, core_send, core_recv, near_send, near_recv, q_sem, w_send, w_recv,
    part_send, part_recv, lse_send, lse_recv, cb_send, cb_recv, ps_send, ps_recv, z_send, z_recv, h_send, h_recv,
):
    b, h, z, xh, c = place()
    up, down = ((b + 4) % 32, h), ((b + 28) % 32, h)
    across, mate = (b + 2 - 4 * xh, h), (b + 1 - 2 * c, h)
    after, before = ((b + 1) % 32, h), ((b + 31) % 32, h)
    g = xh * 2 + c
    y, xl = h // 2, h % 2
    beside, diagonal = (b, h + 1 - 2 * xl), (b + 2 - 4 * xh, h + 1 - 2 * xl)

    loads = [
        local(k_hbm.at[pl.ds(0, PIECE)], kv.at[0, 0, c, 0], load.at[0]),
        local(v_hbm.at[pl.ds(0, PIECE)], kv.at[0, 0, c, 1], load.at[1]),
        local(k_hbm.at[pl.ds(PIECE, PIECE)], kv.at[0, 1, c, 0], load.at[2]),
        local(v_hbm.at[pl.ds(PIECE, PIECE)], kv.at[0, 1, c, 1], load.at[3]),
        local(q_hbm, q_ref, load.at[4]),
        local(rk_hbm, near.at[0, 1], load.at[5]),
        local(rv_hbm, near.at[1, 1], load.at[6]),
        local(seg_hbm, seg_ref, load.at[7]),
        local(w_hbm, wg.at[0, g], load.at[8]),
    ]
    for copy in loads:
        copy.start()

    barrier = pltpu.get_barrier_semaphore()
    partners = [across, diagonal, mate, after, before]
    partners += [((b + 4 * n) % 32, h) for n in range(1, 8)] + [(b, (h + n) % 8) for n in range(1, 8)]
    for device in partners:
        pl.semaphore_signal(barrier, inc=1, device_id=device, device_id_type=MESH)
    pl.semaphore_wait(barrier, len(partners))

    def ring(buf, send, recv, u, d):
        def go(src):
            return remote(src, buf(u, d), send.at[u, d], recv.at[u, d], (up, down)[d])

        return go

    def kv_at(u, d):
        return kv.at[u, d, c]

    def cb_at(u, d):
        return cb.at[u, d]

    def pass_on(at, send, recv, u):
        for d in (0, 1):
            waited(at(u, d), recv.at[u, d])

            @pl.when(u <= 4)
            def _():
                ring(at, send, recv, u + 2, d)(at(u, d)).start()

            @pl.when(u == 5 + d)
            def _():
                ring(at, send, recv, 7, d)(at(u, d)).start()

    def begin(at, send, recv, piece):
        for d in (0, 1):
            ring(at, send, recv, 1 + piece, d)(at(0, piece)).start()

    def all_sent(at, send, recv):
        for u in range(1, 8):
            for d in (0, 1):
                ring(at, send, recv, u, d)(at(u, d)).wait_send()

    def to_mate(u, d):
        return remote(kv_at(u, d), kv_at(u, d), core_send.at[u, d], core_recv.at[u, d], mate)

    send_q = remote(q_hbm, q_other, q_sem.at[0], q_sem.at[1], across)
    send_nk = remote(rk_hbm, near.at[0, 0], near_send.at[0], near_recv.at[0], after)
    send_nv = remote(rv_hbm, near.at[1, 0], near_send.at[1], near_recv.at[1], after)
    def spread_w(k):
        source, dest = wg.at[0, g], wg.at[(0, 1, 1)[k], g]
        return remote(source, dest, w_send.at[k], w_recv.at[k], (across, diagonal, beside)[k])

    g_across = 2 - 2 * xh + c

    def mate_w(k):
        buf = wg.at[(0, 1, 1, 0)[k], (g_across, g_across, g, g)[k]]
        return remote(buf, buf, w_send.at[3 + k], w_recv.at[3 + k], mate)

    def send_part(part, s):
        rows = pl.ds(s * 2 * ROWS, 2 * ROWS)
        device = (across, diagonal, beside)[part]
        return remote(
            part_out.at[part, rows], part_in.at[part, rows], part_send.at[part, s], part_recv.at[part, s], device
        )

    def send_lse(part):
        return remote(
            lse_out.at[part], lse_in.at[part], lse_send.at[part], lse_recv.at[part], (across, diagonal, beside)[part]
        )

    send_q.start()
    send_nk.start()
    send_nv.start()
    loads[0].wait()
    loads[1].wait()
    begin(kv_at, ring_send, ring_recv, 0)
    loads[2].wait()
    loads[3].wait()
    begin(kv_at, ring_send, ring_recv, 1)
    to_mate(0, 0).start()
    to_mate(0, 1).start()
    for copy in loads[4:]:
        copy.wait()

    for n in range(GROUP):
        for p in (0, 1):
            qs[pl.ds(p * 512 + n * SIDE, SIDE), :] = q_ref[p * SIDE : (p + 1) * SIDE, n * WIDTH : (n + 1) * WIDTH]
    for t_ref, a_ref in ((top, acc), (top_x, acc_x)):
        t_ref[...] = jnp.full((HALF, WIDTH), -1e30, F32)
        a_ref[...] = jnp.zeros((HALF, 2 * WIDTH), F32)

    own_ids = seg_ref[pl.ds(b, 1), :].astype(F32)
    before_ids = seg_ref[pl.ds(jnp.maximum(b - 1, 0), 1), :].astype(F32)
    row_ids = jnp.transpose(jnp.broadcast_to(own_ids, (ROWS, ROWS)))
    row = lax.broadcasted_iota(jnp.int32, (ROWS, ROWS), 0)
    column = lax.broadcasted_iota(jnp.int32, (ROWS, ROWS), 1)
    allow_own = (row_ids == jnp.broadcast_to(own_ids, (ROWS, ROWS))) & (column <= row)
    first = jnp.broadcast_to(b, (ROWS, ROWS)) > 0
    allow_before = (row_ids == jnp.broadcast_to(before_ids, (ROWS, ROWS))) & first
    allowed = jnp.concatenate([jnp.where(allow_before, 1.0, 0.0), jnp.where(allow_own, 1.0, 0.0)], axis=1)
    allowed = [jnp.concatenate([allowed[p * SIDE : (p + 1) * SIDE]] * 2, axis=0) > 0.5 for p in (0, 1)]
    own, partner = (qs, top, acc), (qs_x, top_x, acc_x)

    def tile(refs, n, keys, values, allow=None):
        q, t, total = refs
        rows = pl.ds(n, ROWS) if isinstance(n, int) else pl.ds(pl.multiple_of(n, ROWS), ROWS)
        s = dot_t(q[rows, :], keys)
        if allow is not None:
            s = jnp.where(allow, s, -1e30)
        old = t[rows, :]
        new = jnp.maximum(old, jnp.max(s, axis=1, keepdims=True) * SCALE)
        shrink = jnp.exp2(old - new)
        p = jnp.exp2(s * SCALE - new[:, :1])
        if allow is not None:
            p = jnp.where(allow, p, 0.0)
        total[rows, :] = total[rows, :] * both(shrink) + jnp.dot(p.astype(BF16), values, preferred_element_type=F32)
        t[rows, :] = new

    eye = row == column

    def unit(u):
        keys = kv[u, :, :, 0].reshape(4 * PIECE, WIDTH)
        return keys, with_ones(kv[u, :, :, 1].reshape(4 * PIECE, WIDTH))

    def from_mate(u):
        for d in (0, 1):
            waited(kv.at[u, d, 1 - c], core_recv.at[u, d])

    def receive(u):
        pass_on(kv_at, ring_send, ring_recv, u)
        to_mate(u, 0).start()
        to_mate(u, 1).start()

    def step(t, _):
        u = jnp.where(t <= 1, 0, jnp.where(t <= 2, 1, t - 3))

        @pl.when((t == 0) | (t == 2) | (t >= 5))
        def _():
            from_mate(u)

        @pl.when(t == 1)
        def _():
            send_nk.wait_recv()
            send_nv.wait_recv()
            near_k = near[0].reshape(2 * ROWS, WIDTH)
            near_v = with_ones(near[1].reshape(2 * ROWS, WIDTH))
            for n in range(GROUP):
                tile(own, n * ROWS, near_k, near_v, allowed[n // 4])

        @pl.when((t == 0) | (t == 2))
        def _():
            keys, values = unit(u)
            for n in range(GROUP):
                tile(own, n * ROWS, keys, values)

        @pl.when((t == 3) | (t == 4))
        def _():
            keys, values = unit(u)
            for n in range(GROUP):
                tile(partner, n * ROWS, keys, values)

        @pl.when((t >= 5) & (t <= 9))
        def _():
            keys, values = unit(u)
            for n in range(GROUP):
                tile(partner, n * ROWS, keys, values)
                tile(own, n * ROWS, keys, values)

        @pl.when(t == 10)
        def _():
            keys, values = unit(u)
            for part in (0, 1, 2):
                refs = (partner, partner, own)[part]
                base = xl * 512 if part == 0 else (1 - xl) * 512
                for n in range(4):
                    tile(refs, base + n * ROWS, keys, values)
                for n in range(4):
                    rows = pl.ds(pl.multiple_of(base + n * ROWS, ROWS), ROWS)
                    total = refs[2][rows, WIDTH:]
                    part_out[part, pl.ds(n * ROWS, ROWS), :] = (refs[2][rows, :WIDTH] / total).astype(BF16)
                    lse = refs[1][rows, :] + jnp.log2(total)
                    lse_out[part, pl.ds(n, 1), :] = jnp.sum(jnp.where(eye, lse, 0.0), axis=0, keepdims=True)
                    if n % 2 == 1:
                        send_part(part, n // 2).start()
                send_lse(part).start()
            spread_w(0).wait_recv()
            mate_w(0).start()
            for n in range(4):
                tile(own, xl * 512 + n * ROWS, keys, values)

        @pl.when((t == 1) | (t == 2))
        def _():
            receive(t)

        @pl.when(t == 1)
        def _():
            for k in (2, 1, 0):
                spread_w(k).start()
            mate_w(3).start()

        @pl.when(t == 2)
        def _():
            send_q.wait_recv()
            for n in range(GROUP):
                for p in (0, 1):
                    x = q_other[p * SIDE : (p + 1) * SIDE, n * WIDTH : (n + 1) * WIDTH]
                    qs_x[pl.ds(p * 512 + n * SIDE, SIDE), :] = x

        @pl.when((t == 4) | (t == 6))
        def _():
            receive(t - 1)
            receive(t)

        @pl.when(t == 8)
        def _():
            receive(7)
            for k in (1, 2):
                spread_w(k).wait_recv()
                mate_w(k).start()

        return 0

    lax.fori_loop(0, 11, step, 0)

    def column(part, n):
        return jnp.transpose(jnp.broadcast_to(lse_in[part, pl.ds(n, 1), :], (ROWS, ROWS)))

    def mix(piece, n, o, lse, part):
        there = column(part, n)
        high = jnp.maximum(lse, there)
        a, d = jnp.exp2(lse - high), jnp.exp2(there - high)
        mixed = o * a + part_in[part, pl.ds(n * ROWS, ROWS), :].astype(F32) * d
        mixed = (mixed / (a + d)).astype(BF16)
        cb[0, piece, :, 2 * n * WIDTH : (2 * n + 1) * WIDTH] = mixed[:SIDE]
        cb[0, piece, :, (2 * n + 1) * WIDTH : (2 * n + 2) * WIDTH] = mixed[SIDE:]

    def received(part):
        send_part(part, 0).wait_recv()
        send_part(part, 1).wait_recv()
        send_lse(part).wait_recv()

    received(0)
    for n in range(4):
        rows = pl.ds(pl.multiple_of(xl * 512 + n * ROWS, ROWS), ROWS)
        total = acc[rows, WIDTH:]
        mix(0, n, acc[rows, :WIDTH] / total, top[rows, :] + jnp.log2(total), 0)
    begin(cb_at, cb_send, cb_recv, 0)
    received(1)
    received(2)
    for n in range(4):
        mix(1, n, part_in[1, pl.ds(n * ROWS, ROWS), :].astype(F32), column(1, n), 2)
    begin(cb_at, cb_send, cb_recv, 1)

    for k in range(4):
        mate_w(k).wait_recv()

    def partial_to(k, there):
        return remote(ps.at[k, there], pr.at[k, y], ps_send.at[k, there], ps_recv.at[k, y], (b, there * 2 + xl))

    def each_y(act):
        for n in range(1, 4):
            act((y + n) % 4)

    def alone(k, u):
        for n in (2, 1, 3, 0):
            q = (y + n) % 4
            value = jnp.dot(cb[u, 0], wg[0, q], preferred_element_type=F32)
            value = value + jnp.dot(cb[u, 1], wg[1, q], preferred_element_type=F32)
            ps[k, q, 0] = value.astype(BF16)
            ps[k, q, 1] = jnp.zeros((SIDE, 256), BF16)
            if n:
                partial_to(k, q).start()

    def to_z(k, d):
        there = (z + k * (2 * d - 1) + 8) % 8
        return remote(red.at[k, d], zr.at[z], z_send.at[k, d], z_recv.at[z], (there * 4 + g, h))

    def sum_up(k):
        each_y(lambda there: waited(pr.at[k, there], ps_recv.at[k, there]))
        value = ps[k, y].astype(F32)
        for n in range(1, 4):
            value = value + pr[k, (y + n) % 4].astype(F32)
        red[k] = value.astype(BF16)

        @pl.when(k > 0)
        def _():
            to_z(k, 0).start()

        @pl.when((k > 0) & (k < 4))
        def _():
            to_z(k, 1).start()

    def out_at(row_half, block):
        rows = pl.ds(pl.multiple_of(row_half * SIDE, SIDE), SIDE)
        return out_ref.at[rows, pl.ds(pl.multiple_of(block * 256, 256), 256)]

    def to_h(buf, there):
        return remote(buf, out_at(xl, y), h_send.at[there], h_recv.at[h], (b, there))

    def hand_over(buf, source):
        @pl.when(source != h)
        def _():
            to_h(buf, source).start()

        @pl.when(source == h)
        def _():
            out_at(xl, y)[...] = buf[...]

    def deliver(k, d):
        source = (z + k * (1 - 2 * d) + 8) % 8
        waited(zr.at[source], z_recv.at[source])
        hand_over(zr.at[source], source)

    alone(0, 0)
    all_sent(kv_at, ring_send, ring_recv)
    for u in range(8):
        for d in (0, 1):
            to_mate(u, d).wait_send()
    send_q.wait_send()
    send_nk.wait_send()
    send_nv.wait_send()
    for k in range(3):
        send_part(k, 0).wait_send()
        send_part(k, 1).wait_send()
        send_lse(k).wait_send()
        spread_w(k).wait_send()
    for k in range(4):
        mate_w(k).wait_send()

    def stage(k, _):
        u = 2 * k - 1
        pass_on(cb_at, cb_send, cb_recv, u)
        rows = cb[u].reshape(ROWS, 1024)
        for q in range(4):
            half_sum[q] = jnp.dot(rows, wg[0, q], preferred_element_type=F32)
        pass_on(cb_at, cb_send, cb_recv, u + 1)
        rows = cb[u + 1].reshape(ROWS, 1024)
        for n in (2, 1, 3, 0):
            q = (y + n) % 4
            value = (half_sum[q] + jnp.dot(rows, wg[1, q], preferred_element_type=F32)).astype(BF16)
            ps[k, q] = value.reshape(2, SIDE, 256)
            if n:
                partial_to(k, q).start()

        @pl.when(k >= 2)
        def _():
            sum_up(k - 1)

        @pl.when(k == 3)
        def _():
            deliver(1, 0)
            deliver(1, 1)

        return 0

    lax.fori_loop(1, 4, stage, 0)
    sum_up(0)
    hand_over(red.at[0, 0], z)
    pass_on(cb_at, cb_send, cb_recv, 7)
    alone(4, 7)
    sum_up(3)
    deliver(2, 0)
    deliver(2, 1)
    sum_up(4)
    deliver(3, 0)
    deliver(3, 1)
    deliver(4, 0)

    for n in range(1, 8):
        source = (h + n) % 8
        waited(out_at(source % 2, source // 2), h_recv.at[source])

    for n in range(8):
        source = (z + n) % 8

        @pl.when(source != h)
        def _():
            to_h(zr.at[source], source).wait_send()

    for k in range(5):
        each_y(lambda there: partial_to(k, there).wait_send())
        if k > 0:
            to_z(k, 0).wait_send()
        if 0 < k < 4:
            to_z(k, 1).wait_send()
    all_sent(cb_at, cb_send, cb_recv)


def on_device(q, k, v, rk, rv, seg, w):
    dma = pltpu.SemaphoreType.DMA
    return pl.pallas_call(
        whole,
        out_shape=jax.ShapeDtypeStruct((ROWS, 1024), BF16),
        in_specs=[ANY] * 7,
        out_specs=VMEM,
        scratch_shapes=[
            pltpu.VMEM((ROWS, HALF), BF16),
            pltpu.VMEM((ROWS, HALF), BF16),
            pltpu.VMEM((HALF, WIDTH), BF16),
            pltpu.VMEM((HALF, WIDTH), BF16),
            pltpu.VMEM((8, 2, 2, 2, PIECE, WIDTH), BF16),
            pltpu.VMEM((2, 2, ROWS, WIDTH), BF16),
            pltpu.VMEM((32, ROWS), jnp.int32),
            pltpu.VMEM((HALF, WIDTH), F32),
            pltpu.VMEM((HALF, WIDTH), F32),
            pltpu.VMEM((HALF, 2 * WIDTH), F32),
            pltpu.VMEM((HALF, 2 * WIDTH), F32),
            pltpu.VMEM((3, 4 * ROWS, WIDTH), BF16),
            pltpu.VMEM((3, 4 * ROWS, WIDTH), BF16),
            pltpu.VMEM((3, 4, ROWS), F32),
            pltpu.VMEM((3, 4, ROWS), F32),
            pltpu.VMEM((2, 4, 1024, 256), BF16),
            pltpu.VMEM((8, 2, SIDE, 1024), BF16),
            pltpu.VMEM((4, ROWS, 256), F32),
            pltpu.VMEM((5, 4, 2, SIDE, 256), BF16),
            pltpu.VMEM((5, 4, 2, SIDE, 256), BF16),
            pltpu.VMEM((5, 2, SIDE, 256), BF16),
            pltpu.VMEM((8, SIDE, 256), BF16),
            dma((9,)),
            dma((8, 2)), dma((8, 2)),
            dma((8, 2)), dma((8, 2)),
            dma((2,)), dma((2,)),
            dma((2,)),
            dma((7,)), dma((7,)),
            dma((3, 2)), dma((3, 2)),
            dma((3,)), dma((3,)),
            dma((8, 2)), dma((8, 2)),
            dma((5, 4)), dma((5, 4)),
            dma((5, 2)), dma((8,)),
            dma((8,)), dma((8,)),
        ],
        compiler_params=pltpu.CompilerParams(
            collective_id=0, has_side_effects=True, vmem_limit_bytes=56 * 2**20
        ),
    )(q, k, v, rk, rv, seg.reshape(32, ROWS), w)


def solution(mesh):
    return jax.shard_map(
        on_device,
        mesh=mesh,
        in_specs=(
            P("blk", "head"),
            P("blk", "head"),
            P("blk", "head"),
            P("blk", "head"),
            P("blk", "head"),
            P(),
            P("head", "blk"),
        ),
        out_specs=P("blk", "head"),
        check_vma=False,
    )
```

```python
import functools
import math

import jax
import jax.numpy as jnp
from jax import lax
from jax.experimental import pallas as pl
from jax.experimental.pallas import tpu as pltpu
from jax.sharding import PartitionSpec as P

WIDTH = 128
ROWS = 128
GROUP = 8
PIECE = 256
SIDE = ROWS // 2
HALF = GROUP * ROWS
SCALE = math.log2(math.e) / math.sqrt(WIDTH)
MESH = pl.DeviceIdType.MESH
F32 = jnp.float32
BF16 = jnp.bfloat16
VMEM = pl.BlockSpec(memory_space=pltpu.VMEM)
ANY = pl.BlockSpec(memory_space=pl.ANY)


def place():
    b, h = lax.axis_index("blk"), lax.axis_index("head")
    return b, h, b // 4, (b // 2) % 2, b % 2


def remote(src, dst, send, recv, device):
    return pltpu.make_async_remote_copy(
        src_ref=src, dst_ref=dst, send_sem=send, recv_sem=recv, device_id=device, device_id_type=MESH
    )


def with_ones(v):
    return jnp.concatenate([v, jnp.ones_like(v)], axis=1)


def dot_t(a, b):
    return lax.dot_general(a, b, (((1,), (1,)), ((), ())), preferred_element_type=F32)


def both(x):
    return jnp.concatenate([x, x], axis=1)


def local(src, dst, sem):
    return pltpu.make_async_copy(src, dst, sem)


def waited(buf, sem):
    pltpu.make_async_copy(buf, buf, sem).wait()


def whole(
    q_hbm, k_hbm, v_hbm, rk_hbm, rv_hbm, seg_hbm, w_hbm,
    out_ref,
    q_ref, q_other, qs, qs_x, kv, near, seg_ref, top, top_x, acc, acc_x, part_out, part_in, lse_out, lse_in,
    wg, cb, half_sum, ps, pr, red, zr,
    load, ring_send, ring_recv, core_send, core_recv, near_send, near_recv, q_sem, w_send, w_recv,
    part_send, part_recv, lse_send, lse_recv, cb_send, cb_recv, ps_send, ps_recv, z_send, z_recv, h_send, h_recv,
):
    b, h, z, xh, c = place()
    up, down = ((b + 4) % 32, h), ((b + 28) % 32, h)
    across, mate = (b + 2 - 4 * xh, h), (b + 1 - 2 * c, h)
    after, before = ((b + 1) % 32, h), ((b + 31) % 32, h)
    g = xh * 2 + c
    y, xl = h // 2, h % 2
    beside, diagonal = (b, h + 1 - 2 * xl), (b + 2 - 4 * xh, h + 1 - 2 * xl)

    loads = [
        local(k_hbm.at[pl.ds(0, PIECE)], kv.at[0, 0, c, 0], load.at[0]),
        local(v_hbm.at[pl.ds(0, PIECE)], kv.at[0, 0, c, 1], load.at[1]),
        local(k_hbm.at[pl.ds(PIECE, PIECE)], kv.at[0, 1, c, 0], load.at[2]),
        local(v_hbm.at[pl.ds(PIECE, PIECE)], kv.at[0, 1, c, 1], load.at[3]),
        local(q_hbm, q_ref, load.at[4]),
        local(rk_hbm, near.at[0, 1], load.at[5]),
        local(rv_hbm, near.at[1, 1], load.at[6]),
        local(seg_hbm, seg_ref, load.at[7]),
        local(w_hbm, wg.at[0, g], load.at[8]),
    ]
    for copy in loads:
        copy.start()

    barrier = pltpu.get_barrier_semaphore()
    partners = [across, diagonal, mate, after, before]
    partners += [((b + 4 * n) % 32, h) for n in range(1, 8)] + [(b, (h + n) % 8) for n in range(1, 8)]
    for device in partners:
        pl.semaphore_signal(barrier, inc=1, device_id=device, device_id_type=MESH)
    pl.semaphore_wait(barrier, len(partners))

    def ring(buf, send, recv, u, d):
        def go(src):
            return remote(src, buf(u, d), send.at[u, d], recv.at[u, d], (up, down)[d])

        return go

    def kv_at(u, d):
        return kv.at[u, d, c]

    def cb_at(u, d):
        return cb.at[u, d]

    def pass_on(at, send, recv, u):
        for d in (0, 1):
            waited(at(u, d), recv.at[u, d])

            @pl.when(u <= 4)
            def _():
                ring(at, send, recv, u + 2, d)(at(u, d)).start()

            @pl.when(u == 5 + d)
            def _():
                ring(at, send, recv, 7, d)(at(u, d)).start()

    def begin(at, send, recv, piece):
        for d in (0, 1):
            ring(at, send, recv, 1 + piece, d)(at(0, piece)).start()

    def all_sent(at, send, recv):
        for u in range(1, 8):
            for d in (0, 1):
                ring(at, send, recv, u, d)(at(u, d)).wait_send()

    def to_mate(u, d):
        return remote(kv_at(u, d), kv_at(u, d), core_send.at[u, d], core_recv.at[u, d], mate)

    send_q = remote(q_hbm, q_other, q_sem.at[0], q_sem.at[1], across)
    send_nk = remote(rk_hbm, near.at[0, 0], near_send.at[0], near_recv.at[0], after)
    send_nv = remote(rv_hbm, near.at[1, 0], near_send.at[1], near_recv.at[1], after)
    def spread_w(k):
        source, dest = wg.at[0, g], wg.at[(0, 1, 1)[k], g]
        return remote(source, dest, w_send.at[k], w_recv.at[k], (across, diagonal, beside)[k])

    g_across = 2 - 2 * xh + c

    def mate_w(k):
        buf = wg.at[(0, 1, 1, 0)[k], (g_across, g_across, g, g)[k]]
        return remote(buf, buf, w_send.at[3 + k], w_recv.at[3 + k], mate)

    def send_part(part, s):
        rows = pl.ds(s * 2 * ROWS, 2 * ROWS)
        device = (across, diagonal, beside)[part]
        return remote(
            part_out.at[part, rows], part_in.at[part, rows], part_send.at[part, s], part_recv.at[part, s], device
        )

    def send_lse(part):
        return remote(
            lse_out.at[part], lse_in.at[part], lse_send.at[part], lse_recv.at[part], (across, diagonal, beside)[part]
        )

    send_q.start()
    send_nk.start()
    send_nv.start()
    loads[0].wait()
    loads[1].wait()
    begin(kv_at, ring_send, ring_recv, 0)
    loads[2].wait()
    loads[3].wait()
    begin(kv_at, ring_send, ring_recv, 1)
    to_mate(0, 0).start()
    to_mate(0, 1).start()
    for copy in loads[4:]:
        copy.wait()

    for n in range(GROUP):
        for p in (0, 1):
            qs[pl.ds(p * 512 + n * SIDE, SIDE), :] = q_ref[p * SIDE : (p + 1) * SIDE, n * WIDTH : (n + 1) * WIDTH]
    for t_ref, a_ref in ((top, acc), (top_x, acc_x)):
        t_ref[...] = jnp.full((HALF, WIDTH), -1e30, F32)
        a_ref[...] = jnp.zeros((HALF, 2 * WIDTH), F32)

    own_ids = seg_ref[pl.ds(b, 1), :].astype(F32)
    before_ids = seg_ref[pl.ds(jnp.maximum(b - 1, 0), 1), :].astype(F32)
    row_ids = jnp.transpose(jnp.broadcast_to(own_ids, (ROWS, ROWS)))
    row = lax.broadcasted_iota(jnp.int32, (ROWS, ROWS), 0)
    column = lax.broadcasted_iota(jnp.int32, (ROWS, ROWS), 1)
    allow_own = (row_ids == jnp.broadcast_to(own_ids, (ROWS, ROWS))) & (column <= row)
    first = jnp.broadcast_to(b, (ROWS, ROWS)) > 0
    allow_before = (row_ids == jnp.broadcast_to(before_ids, (ROWS, ROWS))) & first
    allowed = jnp.concatenate([jnp.where(allow_before, 1.0, 0.0), jnp.where(allow_own, 1.0, 0.0)], axis=1)
    allowed = [jnp.concatenate([allowed[p * SIDE : (p + 1) * SIDE]] * 2, axis=0) > 0.5 for p in (0, 1)]
    own, partner = (qs, top, acc), (qs_x, top_x, acc_x)

    def tile(refs, n, keys, values, allow=None):
        q, t, total = refs
        rows = pl.ds(n, ROWS) if isinstance(n, int) else pl.ds(pl.multiple_of(n, ROWS), ROWS)
        s = dot_t(q[rows, :], keys)
        if allow is not None:
            s = jnp.where(allow, s, -1e30)
        old = t[rows, :]
        new = jnp.maximum(old, jnp.max(s, axis=1, keepdims=True) * SCALE)
        shrink = jnp.exp2(old - new)
        p = jnp.exp2(s * SCALE - new[:, :1])
        if allow is not None:
            p = jnp.where(allow, p, 0.0)
        total[rows, :] = total[rows, :] * both(shrink) + jnp.dot(p.astype(BF16), values, preferred_element_type=F32)
        t[rows, :] = new

    eye = row == column

    def unit(u):
        keys = kv[u, :, :, 0].reshape(4 * PIECE, WIDTH)
        return keys, with_ones(kv[u, :, :, 1].reshape(4 * PIECE, WIDTH))

    def from_mate(u):
        for d in (0, 1):
            waited(kv.at[u, d, 1 - c], core_recv.at[u, d])

    def receive(u):
        pass_on(kv_at, ring_send, ring_recv, u)
        to_mate(u, 0).start()
        to_mate(u, 1).start()

    def step(t, _):
        u = jnp.where(t <= 1, 0, jnp.where(t <= 2, 1, t - 3))

        @pl.when((t == 0) | (t == 2) | (t >= 5))
        def _():
            from_mate(u)

        @pl.when(t == 1)
        def _():
            send_nk.wait_recv()
            send_nv.wait_recv()
            near_k = near[0].reshape(2 * ROWS, WIDTH)
            near_v = with_ones(near[1].reshape(2 * ROWS, WIDTH))
            for n in range(GROUP):
                tile(own, n * ROWS, near_k, near_v, allowed[n // 4])

        @pl.when((t == 0) | (t == 2))
        def _():
            keys, values = unit(u)
            for n in range(GROUP):
                tile(own, n * ROWS, keys, values)

        @pl.when((t == 3) | (t == 4))
        def _():
            keys, values = unit(u)
            for n in range(GROUP):
                tile(partner, n * ROWS, keys, values)

        @pl.when((t >= 5) & (t <= 9))
        def _():
            keys, values = unit(u)
            for n in range(GROUP):
                tile(partner, n * ROWS, keys, values)
                tile(own, n * ROWS, keys, values)

        @pl.when(t == 10)
        def _():
            keys, values = unit(u)
            for part in (0, 1, 2):
                refs = (partner, partner, own)[part]
                base = xl * 512 if part == 0 else (1 - xl) * 512
                for n in range(4):
                    tile(refs, base + n * ROWS, keys, values)
                for n in range(4):
                    rows = pl.ds(pl.multiple_of(base + n * ROWS, ROWS), ROWS)
                    total = refs[2][rows, WIDTH:]
                    part_out[part, pl.ds(n * ROWS, ROWS), :] = (refs[2][rows, :WIDTH] / total).astype(BF16)
                    lse = refs[1][rows, :] + jnp.log2(total)
                    lse_out[part, pl.ds(n, 1), :] = jnp.sum(jnp.where(eye, lse, 0.0), axis=0, keepdims=True)
                    if n % 2 == 1:
                        send_part(part, n // 2).start()
                send_lse(part).start()
            spread_w(0).wait_recv()
            mate_w(0).start()
            for n in range(4):
                tile(own, xl * 512 + n * ROWS, keys, values)

        @pl.when((t == 1) | (t == 2))
        def _():
            receive(t)

        @pl.when(t == 1)
        def _():
            for k in (2, 1, 0):
                spread_w(k).start()
            mate_w(3).start()

        @pl.when(t == 2)
        def _():
            send_q.wait_recv()
            for n in range(GROUP):
                for p in (0, 1):
                    x = q_other[p * SIDE : (p + 1) * SIDE, n * WIDTH : (n + 1) * WIDTH]
                    qs_x[pl.ds(p * 512 + n * SIDE, SIDE), :] = x

        @pl.when((t >= 3) & (t <= 6))
        def _():
            receive(t)

        @pl.when(t == 8)
        def _():
            receive(7)
            for k in (1, 2):
                spread_w(k).wait_recv()
                mate_w(k).start()

        return 0

    lax.fori_loop(0, 11, step, 0)

    def column(part, n):
        return jnp.transpose(jnp.broadcast_to(lse_in[part, pl.ds(n, 1), :], (ROWS, ROWS)))

    def mix(piece, n, o, lse, part):
        there = column(part, n)
        high = jnp.maximum(lse, there)
        a, d = jnp.exp2(lse - high), jnp.exp2(there - high)
        mixed = o * a + part_in[part, pl.ds(n * ROWS, ROWS), :].astype(F32) * d
        mixed = (mixed / (a + d)).astype(BF16)
        cb[0, piece, :, 2 * n * WIDTH : (2 * n + 1) * WIDTH] = mixed[:SIDE]
        cb[0, piece, :, (2 * n + 1) * WIDTH : (2 * n + 2) * WIDTH] = mixed[SIDE:]

    def received(part):
        send_part(part, 0).wait_recv()
        send_part(part, 1).wait_recv()
        send_lse(part).wait_recv()

    received(0)
    for n in range(4):
        rows = pl.ds(pl.multiple_of(xl * 512 + n * ROWS, ROWS), ROWS)
        total = acc[rows, WIDTH:]
        mix(0, n, acc[rows, :WIDTH] / total, top[rows, :] + jnp.log2(total), 0)
    begin(cb_at, cb_send, cb_recv, 0)
    received(1)
    received(2)
    for n in range(4):
        mix(1, n, part_in[1, pl.ds(n * ROWS, ROWS), :].astype(F32), column(1, n), 2)
    begin(cb_at, cb_send, cb_recv, 1)

    for k in range(4):
        mate_w(k).wait_recv()

    def partial_to(k, there):
        return remote(ps.at[k, there], pr.at[k, y], ps_send.at[k, there], ps_recv.at[k, y], (b, there * 2 + xl))

    def each_y(act):
        for n in range(1, 4):
            act((y + n) % 4)

    def block_alone(k, u, q):
        value = jnp.dot(cb[u, 0], wg[0, q], preferred_element_type=F32)
        value = value + jnp.dot(cb[u, 1], wg[1, q], preferred_element_type=F32)
        ps[k, q, 0] = value.astype(BF16)
        ps[k, q, 1] = jnp.zeros((SIDE, 256), BF16)

    def alone(k, u):
        for n in (2, 1, 3, 0):
            q = (y + n) % 4
            block_alone(k, u, q)
            if n:
                partial_to(k, q).start()

    def own_block(k, half):
        @pl.when(k <= 2)
        def _():
            n = jnp.where(k == 1, 2 - half, 3 - 3 * half)
            q = (y + n) % 4
            block_alone(0, 0, q)

            @pl.when(n > 0)
            def _():
                partial_to(0, q).start()

    def to_z(k, d):
        there = (z + k * (2 * d - 1) + 8) % 8
        return remote(red.at[k, d], zr.at[z], z_send.at[k, d], z_recv.at[z], (there * 4 + g, h))

    def sum_up(k):
        each_y(lambda there: waited(pr.at[k, there], ps_recv.at[k, there]))
        value = ps[k, y].astype(F32)
        for n in range(1, 4):
            value = value + pr[k, (y + n) % 4].astype(F32)
        red[k] = value.astype(BF16)

        @pl.when(k > 0)
        def _():
            to_z(k, 0).start()

        @pl.when((k > 0) & (k < 4))
        def _():
            to_z(k, 1).start()

    def out_at(row_half, block):
        rows = pl.ds(pl.multiple_of(row_half * SIDE, SIDE), SIDE)
        return out_ref.at[rows, pl.ds(pl.multiple_of(block * 256, 256), 256)]

    def to_h(buf, there):
        return remote(buf, out_at(xl, y), h_send.at[there], h_recv.at[h], (b, there))

    def hand_over(buf, source):
        @pl.when(source != h)
        def _():
            to_h(buf, source).start()

        @pl.when(source == h)
        def _():
            out_at(xl, y)[...] = buf[...]

    def deliver(k, d):
        source = (z + k * (1 - 2 * d) + 8) % 8
        waited(zr.at[source], z_recv.at[source])
        hand_over(zr.at[source], source)

    all_sent(kv_at, ring_send, ring_recv)
    for u in range(8):
        for d in (0, 1):
            to_mate(u, d).wait_send()
    send_q.wait_send()
    send_nk.wait_send()
    send_nv.wait_send()
    for k in range(3):
        send_part(k, 0).wait_send()
        send_part(k, 1).wait_send()
        send_lse(k).wait_send()
        spread_w(k).wait_send()
    for k in range(4):
        mate_w(k).wait_send()

    def stage(k, _):
        u = 2 * k - 1
        pass_on(cb_at, cb_send, cb_recv, u)
        rows = cb[u].reshape(ROWS, 1024)
        for q in range(4):
            half_sum[q] = jnp.dot(rows, wg[0, q], preferred_element_type=F32)
        own_block(k, 0)
        pass_on(cb_at, cb_send, cb_recv, u + 1)
        rows = cb[u + 1].reshape(ROWS, 1024)
        for n in (2, 1, 3, 0):
            q = (y + n) % 4
            value = (half_sum[q] + jnp.dot(rows, wg[1, q], preferred_element_type=F32)).astype(BF16)
            ps[k, q] = value.reshape(2, SIDE, 256)
            if n:
                partial_to(k, q).start()
        own_block(k, 1)

        @pl.when(k >= 2)
        def _():
            sum_up(k - 1)

        @pl.when(k == 3)
        def _():
            deliver(1, 0)
            deliver(1, 1)

        return 0

    lax.fori_loop(1, 4, stage, 0)
    sum_up(0)
    hand_over(red.at[0, 0], z)
    pass_on(cb_at, cb_send, cb_recv, 7)
    alone(4, 7)
    sum_up(3)
    deliver(2, 0)
    deliver(2, 1)
    sum_up(4)
    deliver(3, 0)
    deliver(3, 1)
    deliver(4, 0)

    for n in range(1, 8):
        source = (h + n) % 8
        waited(out_at(source % 2, source // 2), h_recv.at[source])

    for n in range(8):
        source = (z + n) % 8

        @pl.when(source != h)
        def _():
            to_h(zr.at[source], source).wait_send()

    for k in range(5):
        each_y(lambda there: partial_to(k, there).wait_send())
        if k > 0:
            to_z(k, 0).wait_send()
        if 0 < k < 4:
            to_z(k, 1).wait_send()
    all_sent(cb_at, cb_send, cb_recv)


def on_device(q, k, v, rk, rv, seg, w):
    dma = pltpu.SemaphoreType.DMA
    return pl.pallas_call(
        whole,
        out_shape=jax.ShapeDtypeStruct((ROWS, 1024), BF16),
        in_specs=[ANY] * 7,
        out_specs=VMEM,
        scratch_shapes=[
            pltpu.VMEM((ROWS, HALF), BF16),
            pltpu.VMEM((ROWS, HALF), BF16),
            pltpu.VMEM((HALF, WIDTH), BF16),
            pltpu.VMEM((HALF, WIDTH), BF16),
            pltpu.VMEM((8, 2, 2, 2, PIECE, WIDTH), BF16),
            pltpu.VMEM((2, 2, ROWS, WIDTH), BF16),
            pltpu.VMEM((32, ROWS), jnp.int32),
            pltpu.VMEM((HALF, WIDTH), F32),
            pltpu.VMEM((HALF, WIDTH), F32),
            pltpu.VMEM((HALF, 2 * WIDTH), F32),
            pltpu.VMEM((HALF, 2 * WIDTH), F32),
            pltpu.VMEM((3, 4 * ROWS, WIDTH), BF16),
            pltpu.VMEM((3, 4 * ROWS, WIDTH), BF16),
            pltpu.VMEM((3, 4, ROWS), F32),
            pltpu.VMEM((3, 4, ROWS), F32),
            pltpu.VMEM((2, 4, 1024, 256), BF16),
            pltpu.VMEM((8, 2, SIDE, 1024), BF16),
            pltpu.VMEM((4, ROWS, 256), F32),
            pltpu.VMEM((5, 4, 2, SIDE, 256), BF16),
            pltpu.VMEM((5, 4, 2, SIDE, 256), BF16),
            pltpu.VMEM((5, 2, SIDE, 256), BF16),
            pltpu.VMEM((8, SIDE, 256), BF16),
            dma((9,)),
            dma((8, 2)), dma((8, 2)),
            dma((8, 2)), dma((8, 2)),
            dma((2,)), dma((2,)),
            dma((2,)),
            dma((7,)), dma((7,)),
            dma((3, 2)), dma((3, 2)),
            dma((3,)), dma((3,)),
            dma((8, 2)), dma((8, 2)),
            dma((5, 4)), dma((5, 4)),
            dma((5, 2)), dma((8,)),
            dma((8,)), dma((8,)),
        ],
        compiler_params=pltpu.CompilerParams(
            collective_id=0, has_side_effects=True, vmem_limit_bytes=56 * 2**20
        ),
    )(q, k, v, rk, rv, seg.reshape(32, ROWS), w)


def solution(mesh):
    return jax.shard_map(
        on_device,
        mesh=mesh,
        in_specs=(
            P("blk", "head"),
            P("blk", "head"),
            P("blk", "head"),
            P("blk", "head"),
            P("blk", "head"),
            P(),
            P("head", "blk"),
        ),
        out_specs=P("blk", "head"),
        check_vma=False,
    )
```

```python
import functools
import math

import jax
import jax.numpy as jnp
from jax import lax
from jax.experimental import pallas as pl
from jax.experimental.pallas import tpu as pltpu
from jax.sharding import PartitionSpec as P

WIDTH = 128
ROWS = 128
GROUP = 8
PIECE = 256
SIDE = ROWS // 2
HALF = GROUP * ROWS
SCALE = math.log2(math.e) / math.sqrt(WIDTH)
MESH = pl.DeviceIdType.MESH
F32 = jnp.float32
BF16 = jnp.bfloat16
VMEM = pl.BlockSpec(memory_space=pltpu.VMEM)
ANY = pl.BlockSpec(memory_space=pl.ANY)


def place():
    b, h = lax.axis_index("blk"), lax.axis_index("head")
    return b, h, b // 4, (b // 2) % 2, b % 2


def remote(src, dst, send, recv, device):
    return pltpu.make_async_remote_copy(
        src_ref=src, dst_ref=dst, send_sem=send, recv_sem=recv, device_id=device, device_id_type=MESH
    )


def with_ones(v):
    return jnp.concatenate([v, jnp.ones_like(v)], axis=1)


def dot_t(a, b):
    return lax.dot_general(a, b, (((1,), (1,)), ((), ())), preferred_element_type=F32)


def both(x):
    return jnp.concatenate([x, x], axis=1)


def local(src, dst, sem):
    return pltpu.make_async_copy(src, dst, sem)


def waited(buf, sem):
    pltpu.make_async_copy(buf, buf, sem).wait()


def whole(
    q_hbm, k_hbm, v_hbm, rk_hbm, rv_hbm, seg_hbm, w_hbm,
    out_ref,
    q_ref, q_other, qs, qs_x, kv, near, seg_ref, top, top_x, acc, acc_x, part_out, part_in, lse_out, lse_in,
    wg, cb, half_sum, ps, pr, red, zr,
    load, ring_send, ring_recv, core_send, core_recv, near_send, near_recv, q_sem, w_send, w_recv,
    part_send, part_recv, lse_send, lse_recv, cb_send, cb_recv, ps_send, ps_recv, z_send, z_recv, h_send, h_recv,
):
    b, h, z, xh, c = place()
    up, down = ((b + 4) % 32, h), ((b + 28) % 32, h)
    across, mate = (b + 2 - 4 * xh, h), (b + 1 - 2 * c, h)
    after, before = ((b + 1) % 32, h), ((b + 31) % 32, h)
    g = xh * 2 + c
    y, xl = h // 2, h % 2
    beside, diagonal = (b, h + 1 - 2 * xl), (b + 2 - 4 * xh, h + 1 - 2 * xl)

    loads = [
        local(k_hbm.at[pl.ds(0, PIECE)], kv.at[0, 0, c, 0], load.at[0]),
        local(v_hbm.at[pl.ds(0, PIECE)], kv.at[0, 0, c, 1], load.at[1]),
        local(k_hbm.at[pl.ds(PIECE, PIECE)], kv.at[0, 1, c, 0], load.at[2]),
        local(v_hbm.at[pl.ds(PIECE, PIECE)], kv.at[0, 1, c, 1], load.at[3]),
        local(q_hbm, q_ref, load.at[4]),
        local(rk_hbm, near.at[0, 1], load.at[5]),
        local(rv_hbm, near.at[1, 1], load.at[6]),
        local(seg_hbm, seg_ref, load.at[7]),
        local(w_hbm, wg.at[0, g], load.at[8]),
    ]
    for copy in loads:
        copy.start()

    barrier = pltpu.get_barrier_semaphore()
    partners = [across, diagonal, mate, after, before]
    partners += [((b + 4 * n) % 32, h) for n in range(1, 8)] + [(b, (h + n) % 8) for n in range(1, 8)]
    for device in partners:
        pl.semaphore_signal(barrier, inc=1, device_id=device, device_id_type=MESH)
    for t_ref, a_ref in ((top, acc), (top_x, acc_x)):
        t_ref[...] = jnp.full((HALF, WIDTH), -1e30, F32)
        a_ref[...] = jnp.zeros((HALF, 2 * WIDTH), F32)
    pl.semaphore_wait(barrier, len(partners))

    def ring(buf, send, recv, u, d):
        def go(src):
            return remote(src, buf(u, d), send.at[u, d], recv.at[u, d], (up, down)[d])

        return go

    def kv_at(u, d):
        return kv.at[u, d, c]

    def cb_at(u, d):
        return cb.at[u, d]

    def pass_on(at, send, recv, u):
        for d in (0, 1):
            waited(at(u, d), recv.at[u, d])

            @pl.when(u <= 4)
            def _():
                ring(at, send, recv, u + 2, d)(at(u, d)).start()

            @pl.when(u == 5 + d)
            def _():
                ring(at, send, recv, 7, d)(at(u, d)).start()

    def begin(at, send, recv, piece):
        for d in (0, 1):
            ring(at, send, recv, 1 + piece, d)(at(0, piece)).start()

    def all_sent(at, send, recv):
        for u in range(1, 8):
            for d in (0, 1):
                ring(at, send, recv, u, d)(at(u, d)).wait_send()

    def to_mate(u, d):
        return remote(kv_at(u, d), kv_at(u, d), core_send.at[u, d], core_recv.at[u, d], mate)

    send_q = remote(q_hbm, q_other, q_sem.at[0], q_sem.at[1], across)
    send_nk = remote(rk_hbm, near.at[0, 0], near_send.at[0], near_recv.at[0], after)
    send_nv = remote(rv_hbm, near.at[1, 0], near_send.at[1], near_recv.at[1], after)
    def spread_w(k):
        source, dest = wg.at[0, g], wg.at[(0, 1, 1)[k], g]
        return remote(source, dest, w_send.at[k], w_recv.at[k], (across, diagonal, beside)[k])

    g_across = 2 - 2 * xh + c

    def mate_w(k):
        buf = wg.at[(0, 1, 1, 0)[k], (g_across, g_across, g, g)[k]]
        return remote(buf, buf, w_send.at[3 + k], w_recv.at[3 + k], mate)

    def send_part(part, s):
        rows = pl.ds(s * 2 * ROWS, 2 * ROWS)
        device = (across, diagonal, beside)[part]
        return remote(
            part_out.at[part, rows], part_in.at[part, rows], part_send.at[part, s], part_recv.at[part, s], device
        )

    def send_lse(part):
        return remote(
            lse_out.at[part], lse_in.at[part], lse_send.at[part], lse_recv.at[part], (across, diagonal, beside)[part]
        )

    send_q.start()
    send_nk.start()
    send_nv.start()
    loads[0].wait()
    loads[1].wait()
    begin(kv_at, ring_send, ring_recv, 0)
    loads[2].wait()
    loads[3].wait()
    begin(kv_at, ring_send, ring_recv, 1)
    to_mate(0, 0).start()
    to_mate(0, 1).start()
    for copy in loads[4:8]:
        copy.wait()

    for n in range(GROUP):
        for p in (0, 1):
            qs[pl.ds(p * 512 + n * SIDE, SIDE), :] = q_ref[p * SIDE : (p + 1) * SIDE, n * WIDTH : (n + 1) * WIDTH]

    own_ids = seg_ref[pl.ds(b, 1), :].astype(F32)
    before_ids = seg_ref[pl.ds(jnp.maximum(b - 1, 0), 1), :].astype(F32)
    row_ids = jnp.transpose(jnp.broadcast_to(own_ids, (ROWS, ROWS)))
    row = lax.broadcasted_iota(jnp.int32, (ROWS, ROWS), 0)
    column = lax.broadcasted_iota(jnp.int32, (ROWS, ROWS), 1)
    allow_own = (row_ids == jnp.broadcast_to(own_ids, (ROWS, ROWS))) & (column <= row)
    first = jnp.broadcast_to(b, (ROWS, ROWS)) > 0
    allow_before = (row_ids == jnp.broadcast_to(before_ids, (ROWS, ROWS))) & first
    allowed = jnp.concatenate([jnp.where(allow_before, 1.0, 0.0), jnp.where(allow_own, 1.0, 0.0)], axis=1)
    allowed = [jnp.concatenate([allowed[p * SIDE : (p + 1) * SIDE]] * 2, axis=0) > 0.5 for p in (0, 1)]
    own, partner = (qs, top, acc), (qs_x, top_x, acc_x)

    def tile(refs, n, keys, values, allow=None):
        q, t, total = refs
        rows = pl.ds(n, ROWS) if isinstance(n, int) else pl.ds(pl.multiple_of(n, ROWS), ROWS)
        s = dot_t(q[rows, :], keys)
        if allow is not None:
            s = jnp.where(allow, s, -1e30)
        old = t[rows, :]
        new = jnp.maximum(old, jnp.max(s, axis=1, keepdims=True) * SCALE)
        shrink = jnp.exp2(old - new)
        p = jnp.exp2(s * SCALE - new[:, :1])
        if allow is not None:
            p = jnp.where(allow, p, 0.0)
        total[rows, :] = total[rows, :] * both(shrink) + jnp.dot(p.astype(BF16), values, preferred_element_type=F32)
        t[rows, :] = new

    eye = row == column

    def unit(u):
        keys = kv[u, :, :, 0].reshape(4 * PIECE, WIDTH)
        return keys, with_ones(kv[u, :, :, 1].reshape(4 * PIECE, WIDTH))

    def from_mate(u):
        for d in (0, 1):
            waited(kv.at[u, d, 1 - c], core_recv.at[u, d])

    def receive(u):
        pass_on(kv_at, ring_send, ring_recv, u)
        to_mate(u, 0).start()
        to_mate(u, 1).start()

    def step(t, _):
        u = jnp.where(t <= 1, 0, jnp.where(t <= 2, 1, t - 3))

        @pl.when((t == 0) | (t == 2) | (t >= 5))
        def _():
            from_mate(u)

        @pl.when(t == 1)
        def _():
            send_nk.wait_recv()
            send_nv.wait_recv()
            near_k = near[0].reshape(2 * ROWS, WIDTH)
            near_v = with_ones(near[1].reshape(2 * ROWS, WIDTH))
            for n in range(GROUP):
                tile(own, n * ROWS, near_k, near_v, allowed[n // 4])

        @pl.when((t == 0) | (t == 2))
        def _():
            keys, values = unit(u)
            for n in range(GROUP):
                tile(own, n * ROWS, keys, values)

        @pl.when((t == 3) | (t == 4))
        def _():
            keys, values = unit(u)
            for n in range(GROUP):
                tile(partner, n * ROWS, keys, values)

        @pl.when((t >= 5) & (t <= 9))
        def _():
            keys, values = unit(u)
            for n in range(GROUP):
                tile(partner, n * ROWS, keys, values)
                tile(own, n * ROWS, keys, values)

        @pl.when(t == 10)
        def _():
            keys, values = unit(u)
            for part in (0, 1, 2):
                refs = (partner, partner, own)[part]
                base = xl * 512 if part == 0 else (1 - xl) * 512
                for n in range(4):
                    tile(refs, base + n * ROWS, keys, values)
                for n in range(4):
                    rows = pl.ds(pl.multiple_of(base + n * ROWS, ROWS), ROWS)
                    total = refs[2][rows, WIDTH:]
                    part_out[part, pl.ds(n * ROWS, ROWS), :] = (refs[2][rows, :WIDTH] / total).astype(BF16)
                    lse = refs[1][rows, :] + jnp.log2(total)
                    lse_out[part, pl.ds(n, 1), :] = jnp.sum(jnp.where(eye, lse, 0.0), axis=0, keepdims=True)
                    if n % 2 == 1:
                        send_part(part, n // 2).start()
                send_lse(part).start()
            for n in range(4):
                tile(own, xl * 512 + n * ROWS, keys, values)

        @pl.when((t == 1) | (t == 2))
        def _():
            receive(t)

        @pl.when(t == 1)
        def _():
            loads[8].wait()
            for k in (2, 1, 0):
                spread_w(k).start()
            mate_w(3).start()

        @pl.when(t == 2)
        def _():
            send_q.wait_recv()
            for n in range(GROUP):
                for p in (0, 1):
                    x = q_other[p * SIDE : (p + 1) * SIDE, n * WIDTH : (n + 1) * WIDTH]
                    qs_x[pl.ds(p * 512 + n * SIDE, SIDE), :] = x

        @pl.when((t >= 3) & (t <= 6))
        def _():
            receive(t)

        @pl.when(t == 8)
        def _():
            receive(7)
            for k in (1, 2):
                spread_w(k).wait_recv()
                mate_w(k).start()

        return 0

    lax.fori_loop(0, 11, step, 0)

    def column(part, n):
        return jnp.transpose(jnp.broadcast_to(lse_in[part, pl.ds(n, 1), :], (ROWS, ROWS)))

    def mix(piece, n, o, lse, part):
        there = column(part, n)
        high = jnp.maximum(lse, there)
        a, d = jnp.exp2(lse - high), jnp.exp2(there - high)
        mixed = o * a + part_in[part, pl.ds(n * ROWS, ROWS), :].astype(F32) * d
        mixed = (mixed / (a + d)).astype(BF16)
        cb[0, piece, :, 2 * n * WIDTH : (2 * n + 1) * WIDTH] = mixed[:SIDE]
        cb[0, piece, :, (2 * n + 1) * WIDTH : (2 * n + 2) * WIDTH] = mixed[SIDE:]

    def received(part):
        send_part(part, 0).wait_recv()
        send_part(part, 1).wait_recv()
        send_lse(part).wait_recv()

    received(0)
    for n in range(4):
        rows = pl.ds(pl.multiple_of(xl * 512 + n * ROWS, ROWS), ROWS)
        total = acc[rows, WIDTH:]
        mix(0, n, acc[rows, :WIDTH] / total, top[rows, :] + jnp.log2(total), 0)
    begin(cb_at, cb_send, cb_recv, 0)
    spread_w(0).wait_recv()
    mate_w(0).start()
    received(1)
    received(2)
    for n in range(4):
        mix(1, n, part_in[1, pl.ds(n * ROWS, ROWS), :].astype(F32), column(1, n), 2)
    begin(cb_at, cb_send, cb_recv, 1)

    for k in range(4):
        mate_w(k).wait_recv()

    def partial_to(k, there):
        return remote(ps.at[k, there], pr.at[k, y], ps_send.at[k, there], ps_recv.at[k, y], (b, there * 2 + xl))

    def each_y(act):
        for n in range(1, 4):
            act((y + n) % 4)

    def block_alone(k, u, q):
        value = jnp.dot(cb[u, 0], wg[0, q], preferred_element_type=F32)
        value = value + jnp.dot(cb[u, 1], wg[1, q], preferred_element_type=F32)
        ps[k, q, 0] = value.astype(BF16)
        ps[k, q, 1] = jnp.zeros((SIDE, 256), BF16)

    def own_block(k, half):
        @pl.when(k <= 2)
        def _():
            n = jnp.where(k == 1, 2 - half, 3 - 3 * half)
            q = (y + n) % 4
            block_alone(0, 0, q)

            @pl.when(n > 0)
            def _():
                partial_to(0, q).start()

    def to_z(k, d):
        there = (z + k * (2 * d - 1) + 8) % 8
        return remote(red.at[k, d], zr.at[z], z_send.at[k, d], z_recv.at[z], (there * 4 + g, h))

    def sum_up(k):
        each_y(lambda there: waited(pr.at[k, there], ps_recv.at[k, there]))
        value = ps[k, y].astype(F32)
        for n in range(1, 4):
            value = value + pr[k, (y + n) % 4].astype(F32)
        red[k] = value.astype(BF16)

        @pl.when(k > 0)
        def _():
            to_z(k, 0).start()

        @pl.when((k > 0) & (k < 4))
        def _():
            to_z(k, 1).start()

    def out_at(row_half, block):
        rows = pl.ds(pl.multiple_of(row_half * SIDE, SIDE), SIDE)
        return out_ref.at[rows, pl.ds(pl.multiple_of(block * 256, 256), 256)]

    def to_h(buf, there):
        return remote(buf, out_at(xl, y), h_send.at[there], h_recv.at[h], (b, there))

    def hand_over(buf, source):
        @pl.when(source != h)
        def _():
            to_h(buf, source).start()

        @pl.when(source == h)
        def _():
            out_at(xl, y)[...] = buf[...]

    def deliver(k, d):
        source = (z + k * (1 - 2 * d) + 8) % 8
        waited(zr.at[source], z_recv.at[source])
        hand_over(zr.at[source], source)

    all_sent(kv_at, ring_send, ring_recv)
    for u in range(8):
        for d in (0, 1):
            to_mate(u, d).wait_send()
    send_q.wait_send()
    send_nk.wait_send()
    send_nv.wait_send()
    for k in range(3):
        send_part(k, 0).wait_send()
        send_part(k, 1).wait_send()
        send_lse(k).wait_send()
        spread_w(k).wait_send()
    for k in range(4):
        mate_w(k).wait_send()

    def stage(k, _):
        u = 2 * k - 1
        pass_on(cb_at, cb_send, cb_recv, u)
        rows = cb[u].reshape(ROWS, 1024)
        for q in range(4):
            half_sum[q] = jnp.dot(rows, wg[0, q], preferred_element_type=F32)
        own_block(k, 0)
        pass_on(cb_at, cb_send, cb_recv, u + 1)
        rows = cb[u + 1].reshape(ROWS, 1024)
        for n in (2, 1, 3, 0):
            q = (y + n) % 4
            value = (half_sum[q] + jnp.dot(rows, wg[1, q], preferred_element_type=F32)).astype(BF16)
            ps[k, q] = value.reshape(2, SIDE, 256)
            if n:
                partial_to(k, q).start()
        own_block(k, 1)

        @pl.when(k >= 2)
        def _():
            sum_up(k - 1)

        @pl.when(k == 3)
        def _():
            deliver(1, 0)
            deliver(1, 1)

        return 0

    lax.fori_loop(1, 4, stage, 0)
    sum_up(0)
    hand_over(red.at[0, 0], z)
    waited(cb_at(7, 0), cb_recv.at[7, 0])
    for q in range(4):
        half_sum[q, :SIDE] = jnp.dot(cb[7, 0], wg[0, q], preferred_element_type=F32)
    waited(cb_at(7, 1), cb_recv.at[7, 1])
    for n in (2, 1, 3, 0):
        q = (y + n) % 4
        value = half_sum[q, :SIDE] + jnp.dot(cb[7, 1], wg[1, q], preferred_element_type=F32)
        ps[4, q, 0] = value.astype(BF16)
        ps[4, q, 1] = jnp.zeros((SIDE, 256), BF16)
        if n:
            partial_to(4, q).start()
    sum_up(3)
    deliver(2, 0)
    deliver(2, 1)
    sum_up(4)
    deliver(3, 0)
    deliver(3, 1)
    deliver(4, 0)

    for n in range(1, 8):
        source = (h + n) % 8
        waited(out_at(source % 2, source // 2), h_recv.at[source])

    for n in range(8):
        source = (z + n) % 8

        @pl.when(source != h)
        def _():
            to_h(zr.at[source], source).wait_send()

    for k in range(5):
        each_y(lambda there: partial_to(k, there).wait_send())
        if k > 0:
            to_z(k, 0).wait_send()
        if 0 < k < 4:
            to_z(k, 1).wait_send()
    all_sent(cb_at, cb_send, cb_recv)


def on_device(q, k, v, rk, rv, seg, w):
    dma = pltpu.SemaphoreType.DMA
    return pl.pallas_call(
        whole,
        out_shape=jax.ShapeDtypeStruct((ROWS, 1024), BF16),
        in_specs=[ANY] * 7,
        out_specs=VMEM,
        scratch_shapes=[
            pltpu.VMEM((ROWS, HALF), BF16),
            pltpu.VMEM((ROWS, HALF), BF16),
            pltpu.VMEM((HALF, WIDTH), BF16),
            pltpu.VMEM((HALF, WIDTH), BF16),
            pltpu.VMEM((8, 2, 2, 2, PIECE, WIDTH), BF16),
            pltpu.VMEM((2, 2, ROWS, WIDTH), BF16),
            pltpu.VMEM((32, ROWS), jnp.int32),
            pltpu.VMEM((HALF, WIDTH), F32),
            pltpu.VMEM((HALF, WIDTH), F32),
            pltpu.VMEM((HALF, 2 * WIDTH), F32),
            pltpu.VMEM((HALF, 2 * WIDTH), F32),
            pltpu.VMEM((3, 4 * ROWS, WIDTH), BF16),
            pltpu.VMEM((3, 4 * ROWS, WIDTH), BF16),
            pltpu.VMEM((3, 4, ROWS), F32),
            pltpu.VMEM((3, 4, ROWS), F32),
            pltpu.VMEM((2, 4, 1024, 256), BF16),
            pltpu.VMEM((8, 2, SIDE, 1024), BF16),
            pltpu.VMEM((4, ROWS, 256), F32),
            pltpu.VMEM((5, 4, 2, SIDE, 256), BF16),
            pltpu.VMEM((5, 4, 2, SIDE, 256), BF16),
            pltpu.VMEM((5, 2, SIDE, 256), BF16),
            pltpu.VMEM((8, SIDE, 256), BF16),
            dma((9,)),
            dma((8, 2)), dma((8, 2)),
            dma((8, 2)), dma((8, 2)),
            dma((2,)), dma((2,)),
            dma((2,)),
            dma((7,)), dma((7,)),
            dma((3, 2)), dma((3, 2)),
            dma((3,)), dma((3,)),
            dma((8, 2)), dma((8, 2)),
            dma((5, 4)), dma((5, 4)),
            dma((5, 2)), dma((8,)),
            dma((8,)), dma((8,)),
        ],
        compiler_params=pltpu.CompilerParams(
            collective_id=0, has_side_effects=True, vmem_limit_bytes=56 * 2**20
        ),
    )(q, k, v, rk, rv, seg.reshape(32, ROWS), w)


def solution(mesh):
    return jax.shard_map(
        on_device,
        mesh=mesh,
        in_specs=(
            P("blk", "head"),
            P("blk", "head"),
            P("blk", "head"),
            P("blk", "head"),
            P("blk", "head"),
            P(),
            P("head", "blk"),
        ),
        out_specs=P("blk", "head"),
        check_vma=False,
    )
```

```python
import functools
import math

import jax
import jax.numpy as jnp
from jax import lax
from jax.experimental import pallas as pl
from jax.experimental.pallas import tpu as pltpu
from jax.sharding import PartitionSpec as P

WIDTH = 128
ROWS = 128
GROUP = 8
PIECE = 256
SIDE = ROWS // 2
HALF = GROUP * ROWS
SCALE = math.log2(math.e) / math.sqrt(WIDTH)
MESH = pl.DeviceIdType.MESH
F32 = jnp.float32
BF16 = jnp.bfloat16
VMEM = pl.BlockSpec(memory_space=pltpu.VMEM)
ANY = pl.BlockSpec(memory_space=pl.ANY)


def place():
    b, h = lax.axis_index("blk"), lax.axis_index("head")
    return b, h, b // 4, (b // 2) % 2, b % 2


def remote(src, dst, send, recv, device):
    return pltpu.make_async_remote_copy(
        src_ref=src, dst_ref=dst, send_sem=send, recv_sem=recv, device_id=device, device_id_type=MESH
    )


def with_ones(v):
    return jnp.concatenate([v, jnp.ones_like(v)], axis=1)


def dot_t(a, b):
    return lax.dot_general(a, b, (((1,), (1,)), ((), ())), preferred_element_type=F32)


def both(x):
    return jnp.concatenate([x, x], axis=1)


def local(src, dst, sem):
    return pltpu.make_async_copy(src, dst, sem)


def waited(buf, sem):
    pltpu.make_async_copy(buf, buf, sem).wait()


def whole(
    q_hbm, k_hbm, v_hbm, rk_hbm, rv_hbm, seg_hbm, w_hbm,
    out_ref,
    q_ref, q_other, qs, qs_x, kv, near, seg_ref, top, top_x, acc, acc_x, part_out, part_in, lse_out, lse_in,
    wg, cb, half_sum, ps, pr, red, zr,
    load, ring_send, ring_recv, core_send, core_recv, near_send, near_recv, q_sem, w_send, w_recv,
    part_send, part_recv, lse_send, lse_recv, cb_send, cb_recv, ps_send, ps_recv, z_send, z_recv, h_send, h_recv,
):
    b, h, z, xh, c = place()
    up, down = ((b + 4) % 32, h), ((b + 28) % 32, h)
    across, mate = (b + 2 - 4 * xh, h), (b + 1 - 2 * c, h)
    after, before = ((b + 1) % 32, h), ((b + 31) % 32, h)
    g = xh * 2 + c
    y, xl = h // 2, h % 2
    beside, diagonal = (b, h + 1 - 2 * xl), (b + 2 - 4 * xh, h + 1 - 2 * xl)

    loads = [
        local(k_hbm.at[pl.ds(0, PIECE)], kv.at[0, 0, c, 0], load.at[0]),
        local(v_hbm.at[pl.ds(0, PIECE)], kv.at[0, 0, c, 1], load.at[1]),
        local(k_hbm.at[pl.ds(PIECE, PIECE)], kv.at[0, 1, c, 0], load.at[2]),
        local(v_hbm.at[pl.ds(PIECE, PIECE)], kv.at[0, 1, c, 1], load.at[3]),
        local(q_hbm, q_ref, load.at[4]),
        local(rk_hbm, near.at[0, 1], load.at[5]),
        local(rv_hbm, near.at[1, 1], load.at[6]),
        local(seg_hbm, seg_ref, load.at[7]),
        local(w_hbm, wg.at[0, g], load.at[8]),
    ]
    for copy in loads:
        copy.start()

    barrier = pltpu.get_barrier_semaphore()
    partners = [across, diagonal, mate, after, before]
    partners += [((b + 4 * n) % 32, h) for n in range(1, 8)] + [(b, (h + n) % 8) for n in range(1, 8)]
    for device in partners:
        pl.semaphore_signal(barrier, inc=1, device_id=device, device_id_type=MESH)
    for t_ref, a_ref in ((top, acc), (top_x, acc_x)):
        t_ref[...] = jnp.full((HALF, WIDTH), -1e30, F32)
        a_ref[...] = jnp.zeros((HALF, 2 * WIDTH), F32)
    pl.semaphore_wait(barrier, len(partners))

    def ring(buf, send, recv, u, d):
        def go(src):
            return remote(src, buf(u, d), send.at[u, d], recv.at[u, d], (up, down)[d])

        return go

    def kv_at(u, d):
        return kv.at[u, d, c]

    def cb_at(u, d):
        return cb.at[u, d]

    def pass_on(at, send, recv, u):
        for d in (0, 1):
            waited(at(u, d), recv.at[u, d])

            @pl.when(u <= 4)
            def _():
                ring(at, send, recv, u + 2, d)(at(u, d)).start()

            @pl.when(u == 5 + d)
            def _():
                ring(at, send, recv, 7, d)(at(u, d)).start()

    def begin(at, send, recv, piece):
        for d in (0, 1):
            ring(at, send, recv, 1 + piece, d)(at(0, piece)).start()

    def all_sent(at, send, recv):
        for u in range(1, 8):
            for d in (0, 1):
                ring(at, send, recv, u, d)(at(u, d)).wait_send()

    def to_mate(u, d):
        return remote(kv_at(u, d), kv_at(u, d), core_send.at[u, d], core_recv.at[u, d], mate)

    send_q = remote(q_hbm, q_other, q_sem.at[0], q_sem.at[1], across)
    send_nk = remote(rk_hbm, near.at[0, 0], near_send.at[0], near_recv.at[0], after)
    send_nv = remote(rv_hbm, near.at[1, 0], near_send.at[1], near_recv.at[1], after)
    def spread_w(k):
        source, dest = wg.at[0, g], wg.at[(0, 1, 1)[k], g]
        return remote(source, dest, w_send.at[k], w_recv.at[k], (across, diagonal, beside)[k])

    g_across = 2 - 2 * xh + c

    def mate_w(k):
        buf = wg.at[(0, 1, 1, 0)[k], (g_across, g_across, g, g)[k]]
        return remote(buf, buf, w_send.at[3 + k], w_recv.at[3 + k], mate)

    def send_part(part, s):
        rows = pl.ds(s * 2 * ROWS, 2 * ROWS)
        device = (across, diagonal, beside)[part]
        return remote(
            part_out.at[part, rows], part_in.at[part, rows], part_send.at[part, s], part_recv.at[part, s], device
        )

    def send_lse(part):
        return remote(
            lse_out.at[part], lse_in.at[part], lse_send.at[part], lse_recv.at[part], (across, diagonal, beside)[part]
        )

    send_q.start()
    send_nk.start()
    send_nv.start()
    loads[0].wait()
    loads[1].wait()
    begin(kv_at, ring_send, ring_recv, 0)
    loads[2].wait()
    loads[3].wait()
    begin(kv_at, ring_send, ring_recv, 1)
    to_mate(0, 0).start()
    to_mate(0, 1).start()
    for copy in loads[4:8]:
        copy.wait()

    for n in range(GROUP):
        for p in (0, 1):
            qs[pl.ds(p * 512 + n * SIDE, SIDE), :] = q_ref[p * SIDE : (p + 1) * SIDE, n * WIDTH : (n + 1) * WIDTH]

    own_ids = seg_ref[pl.ds(b, 1), :].astype(F32)
    before_ids = seg_ref[pl.ds(jnp.maximum(b - 1, 0), 1), :].astype(F32)
    row_ids = jnp.transpose(jnp.broadcast_to(own_ids, (ROWS, ROWS)))
    row = lax.broadcasted_iota(jnp.int32, (ROWS, ROWS), 0)
    column = lax.broadcasted_iota(jnp.int32, (ROWS, ROWS), 1)
    allow_own = (row_ids == jnp.broadcast_to(own_ids, (ROWS, ROWS))) & (column <= row)
    first = jnp.broadcast_to(b, (ROWS, ROWS)) > 0
    allow_before = (row_ids == jnp.broadcast_to(before_ids, (ROWS, ROWS))) & first
    allowed = jnp.concatenate([jnp.where(allow_before, 1.0, 0.0), jnp.where(allow_own, 1.0, 0.0)], axis=1)
    allowed = [jnp.concatenate([allowed[p * SIDE : (p + 1) * SIDE]] * 2, axis=0) > 0.5 for p in (0, 1)]
    own, partner = (qs, top, acc), (qs_x, top_x, acc_x)

    def tile(refs, n, keys, values, allow=None):
        q, t, total = refs
        rows = pl.ds(n, ROWS) if isinstance(n, int) else pl.ds(pl.multiple_of(n, ROWS), ROWS)
        s = dot_t(q[rows, :], keys)
        if allow is not None:
            s = jnp.where(allow, s, -1e30)
        old = t[rows, :]
        new = jnp.maximum(old, jnp.max(s, axis=1, keepdims=True) * SCALE)
        shrink = jnp.exp2(old - new)
        p = jnp.exp2(s * SCALE - new[:, :1])
        if allow is not None:
            p = jnp.where(allow, p, 0.0)
        total[rows, :] = total[rows, :] * both(shrink) + jnp.dot(p.astype(BF16), values, preferred_element_type=F32)
        t[rows, :] = new

    eye = row == column

    def unit(u):
        keys = kv[u, :, :, 0].reshape(4 * PIECE, WIDTH)
        return keys, with_ones(kv[u, :, :, 1].reshape(4 * PIECE, WIDTH))

    def from_mate(u):
        for d in (0, 1):
            waited(kv.at[u, d, 1 - c], core_recv.at[u, d])

    def receive(u):
        pass_on(kv_at, ring_send, ring_recv, u)
        to_mate(u, 0).start()
        to_mate(u, 1).start()

    def step(t, _):
        u = jnp.where(t <= 1, 0, jnp.where(t <= 2, 1, t - 3))

        @pl.when((t == 0) | (t == 2) | (t >= 5))
        def _():
            from_mate(u)

        @pl.when(t == 1)
        def _():
            send_nk.wait_recv()
            send_nv.wait_recv()
            near_k = near[0].reshape(2 * ROWS, WIDTH)
            near_v = with_ones(near[1].reshape(2 * ROWS, WIDTH))
            for n in range(GROUP):
                tile(own, n * ROWS, near_k, near_v, allowed[n // 4])

        @pl.when((t == 0) | (t == 2))
        def _():
            keys, values = unit(u)
            for n in range(GROUP):
                tile(own, n * ROWS, keys, values)

        @pl.when((t == 3) | (t == 4))
        def _():
            keys, values = unit(u)
            for n in range(GROUP):
                tile(partner, n * ROWS, keys, values)

        @pl.when((t >= 5) & (t <= 9))
        def _():
            keys, values = unit(u)
            for n in range(GROUP):
                tile(partner, n * ROWS, keys, values)
                tile(own, n * ROWS, keys, values)

        @pl.when(t == 10)
        def _():
            keys, values = unit(u)
            for part in (0, 1, 2):
                refs = (partner, partner, own)[part]
                base = xl * 512 if part == 0 else (1 - xl) * 512
                for n in range(4):
                    tile(refs, base + n * ROWS, keys, values)
                for n in range(4):
                    rows = pl.ds(pl.multiple_of(base + n * ROWS, ROWS), ROWS)
                    total = refs[2][rows, WIDTH:]
                    part_out[part, pl.ds(n * ROWS, ROWS), :] = (refs[2][rows, :WIDTH] / total).astype(BF16)
                    lse = refs[1][rows, :] + jnp.log2(total)
                    lse_out[part, pl.ds(n, 1), :] = jnp.sum(jnp.where(eye, lse, 0.0), axis=0, keepdims=True)
                    if n % 2 == 1:
                        send_part(part, n // 2).start()
                send_lse(part).start()
            for n in range(4):
                tile(own, xl * 512 + n * ROWS, keys, values)

        @pl.when((t == 1) | (t == 2))
        def _():
            receive(t)

        @pl.when(t == 1)
        def _():
            loads[8].wait()
            for k in (2, 1, 0):
                spread_w(k).start()
            mate_w(3).start()

        @pl.when(t == 2)
        def _():
            send_q.wait_recv()
            for n in range(GROUP):
                for p in (0, 1):
                    x = q_other[p * SIDE : (p + 1) * SIDE, n * WIDTH : (n + 1) * WIDTH]
                    qs_x[pl.ds(p * 512 + n * SIDE, SIDE), :] = x

        @pl.when((t >= 3) & (t <= 6))
        def _():
            receive(t)

        @pl.when(t == 8)
        def _():
            receive(7)

        return 0

    lax.fori_loop(0, 11, step, 0)

    def column(part, n):
        return jnp.transpose(jnp.broadcast_to(lse_in[part, pl.ds(n, 1), :], (ROWS, ROWS)))

    def mix(piece, n, o, lse, part):
        there = column(part, n)
        high = jnp.maximum(lse, there)
        a, d = jnp.exp2(lse - high), jnp.exp2(there - high)
        mixed = o * a + part_in[part, pl.ds(n * ROWS, ROWS), :].astype(F32) * d
        mixed = (mixed / (a + d)).astype(BF16)
        cb[0, piece, :, 2 * n * WIDTH : (2 * n + 1) * WIDTH] = mixed[:SIDE]
        cb[0, piece, :, (2 * n + 1) * WIDTH : (2 * n + 2) * WIDTH] = mixed[SIDE:]

    def received(part):
        send_part(part, 0).wait_recv()
        send_part(part, 1).wait_recv()
        send_lse(part).wait_recv()

    received(0)
    for n in range(4):
        rows = pl.ds(pl.multiple_of(xl * 512 + n * ROWS, ROWS), ROWS)
        total = acc[rows, WIDTH:]
        mix(0, n, acc[rows, :WIDTH] / total, top[rows, :] + jnp.log2(total), 0)
    begin(cb_at, cb_send, cb_recv, 0)
    for k in range(3):
        spread_w(k).wait_recv()
        mate_w(k).start()
    received(1)
    received(2)
    for n in range(4):
        mix(1, n, part_in[1, pl.ds(n * ROWS, ROWS), :].astype(F32), column(1, n), 2)
    begin(cb_at, cb_send, cb_recv, 1)

    for k in range(4):
        mate_w(k).wait_recv()

    def partial_to(k, there):
        return remote(ps.at[k, there], pr.at[k, y], ps_send.at[k, there], ps_recv.at[k, y], (b, there * 2 + xl))

    def each_y(act):
        for n in range(1, 4):
            act((y + n) % 4)

    def block_alone(k, u, q):
        value = jnp.dot(cb[u, 0], wg[0, q], preferred_element_type=F32)
        value = value + jnp.dot(cb[u, 1], wg[1, q], preferred_element_type=F32)
        ps[k, q, 0] = value.astype(BF16)
        ps[k, q, 1] = jnp.zeros((SIDE, 256), BF16)

    def own_block(k, half):
        @pl.when(k <= 2)
        def _():
            n = jnp.where(k == 1, 2 - half, 3 - 3 * half)
            q = (y + n) % 4
            block_alone(0, 0, q)

            @pl.when(n > 0)
            def _():
                partial_to(0, q).start()

    def to_z(k, d):
        there = (z + k * (2 * d - 1) + 8) % 8
        return remote(red.at[k, d], zr.at[z], z_send.at[k, d], z_recv.at[z], (there * 4 + g, h))

    def sum_up(k):
        each_y(lambda there: waited(pr.at[k, there], ps_recv.at[k, there]))
        value = ps[k, y].astype(F32)
        for n in range(1, 4):
            value = value + pr[k, (y + n) % 4].astype(F32)
        red[k] = value.astype(BF16)

        @pl.when(k > 0)
        def _():
            to_z(k, 0).start()

        @pl.when((k > 0) & (k < 4))
        def _():
            to_z(k, 1).start()

    def out_at(row_half, block):
        rows = pl.ds(pl.multiple_of(row_half * SIDE, SIDE), SIDE)
        return out_ref.at[rows, pl.ds(pl.multiple_of(block * 256, 256), 256)]

    def to_h(buf, there):
        return remote(buf, out_at(xl, y), h_send.at[there], h_recv.at[h], (b, there))

    def hand_over(buf, source):
        @pl.when(source != h)
        def _():
            to_h(buf, source).start()

        @pl.when(source == h)
        def _():
            out_at(xl, y)[...] = buf[...]

    def deliver(k, d):
        source = (z + k * (1 - 2 * d) + 8) % 8
        waited(zr.at[source], z_recv.at[source])
        hand_over(zr.at[source], source)

    all_sent(kv_at, ring_send, ring_recv)
    for u in range(8):
        for d in (0, 1):
            to_mate(u, d).wait_send()
    send_q.wait_send()
    send_nk.wait_send()
    send_nv.wait_send()
    for k in range(3):
        send_part(k, 0).wait_send()
        send_part(k, 1).wait_send()
        send_lse(k).wait_send()
        spread_w(k).wait_send()
    for k in range(4):
        mate_w(k).wait_send()

    def stage(k, _):
        u = 2 * k - 1
        pass_on(cb_at, cb_send, cb_recv, u)
        rows = cb[u].reshape(ROWS, 1024)
        for q in range(4):
            half_sum[q] = jnp.dot(rows, wg[0, q], preferred_element_type=F32)
        own_block(k, 0)
        pass_on(cb_at, cb_send, cb_recv, u + 1)
        rows = cb[u + 1].reshape(ROWS, 1024)
        for n in (2, 1, 3, 0):
            q = (y + n) % 4
            value = (half_sum[q] + jnp.dot(rows, wg[1, q], preferred_element_type=F32)).astype(BF16)
            ps[k, q] = value.reshape(2, SIDE, 256)
            if n:
                partial_to(k, q).start()
        own_block(k, 1)

        @pl.when(k >= 2)
        def _():
            sum_up(k - 1)

        @pl.when(k == 3)
        def _():
            deliver(1, 0)
            deliver(1, 1)

        return 0

    lax.fori_loop(1, 4, stage, 0)
    sum_up(0)
    hand_over(red.at[0, 0], z)
    waited(cb_at(7, 0), cb_recv.at[7, 0])
    for q in range(4):
        half_sum[q, :SIDE] = jnp.dot(cb[7, 0], wg[0, q], preferred_element_type=F32)
    waited(cb_at(7, 1), cb_recv.at[7, 1])
    for n in (2, 1, 3, 0):
        q = (y + n) % 4
        value = half_sum[q, :SIDE] + jnp.dot(cb[7, 1], wg[1, q], preferred_element_type=F32)
        ps[4, q, 0] = value.astype(BF16)
        ps[4, q, 1] = jnp.zeros((SIDE, 256), BF16)
        if n:
            partial_to(4, q).start()
    sum_up(3)
    deliver(2, 0)
    deliver(2, 1)
    sum_up(4)
    deliver(3, 0)
    deliver(3, 1)
    deliver(4, 0)

    for n in range(1, 8):
        source = (h + n) % 8
        waited(out_at(source % 2, source // 2), h_recv.at[source])

    for n in range(8):
        source = (z + n) % 8

        @pl.when(source != h)
        def _():
            to_h(zr.at[source], source).wait_send()

    for k in range(5):
        each_y(lambda there: partial_to(k, there).wait_send())
        if k > 0:
            to_z(k, 0).wait_send()
        if 0 < k < 4:
            to_z(k, 1).wait_send()
    all_sent(cb_at, cb_send, cb_recv)


def on_device(q, k, v, rk, rv, seg, w):
    dma = pltpu.SemaphoreType.DMA
    return pl.pallas_call(
        whole,
        out_shape=jax.ShapeDtypeStruct((ROWS, 1024), BF16),
        in_specs=[ANY] * 7,
        out_specs=VMEM,
        scratch_shapes=[
            pltpu.VMEM((ROWS, HALF), BF16),
            pltpu.VMEM((ROWS, HALF), BF16),
            pltpu.VMEM((HALF, WIDTH), BF16),
            pltpu.VMEM((HALF, WIDTH), BF16),
            pltpu.VMEM((8, 2, 2, 2, PIECE, WIDTH), BF16),
            pltpu.VMEM((2, 2, ROWS, WIDTH), BF16),
            pltpu.VMEM((32, ROWS), jnp.int32),
            pltpu.VMEM((HALF, WIDTH), F32),
            pltpu.VMEM((HALF, WIDTH), F32),
            pltpu.VMEM((HALF, 2 * WIDTH), F32),
            pltpu.VMEM((HALF, 2 * WIDTH), F32),
            pltpu.VMEM((3, 4 * ROWS, WIDTH), BF16),
            pltpu.VMEM((3, 4 * ROWS, WIDTH), BF16),
            pltpu.VMEM((3, 4, ROWS), F32),
            pltpu.VMEM((3, 4, ROWS), F32),
            pltpu.VMEM((2, 4, 1024, 256), BF16),
            pltpu.VMEM((8, 2, SIDE, 1024), BF16),
            pltpu.VMEM((4, ROWS, 256), F32),
            pltpu.VMEM((5, 4, 2, SIDE, 256), BF16),
            pltpu.VMEM((5, 4, 2, SIDE, 256), BF16),
            pltpu.VMEM((5, 2, SIDE, 256), BF16),
            pltpu.VMEM((8, SIDE, 256), BF16),
            dma((9,)),
            dma((8, 2)), dma((8, 2)),
            dma((8, 2)), dma((8, 2)),
            dma((2,)), dma((2,)),
            dma((2,)),
            dma((7,)), dma((7,)),
            dma((3, 2)), dma((3, 2)),
            dma((3,)), dma((3,)),
            dma((8, 2)), dma((8, 2)),
            dma((5, 4)), dma((5, 4)),
            dma((5, 2)), dma((8,)),
            dma((8,)), dma((8,)),
        ],
        compiler_params=pltpu.CompilerParams(
            collective_id=0, has_side_effects=True, vmem_limit_bytes=56 * 2**20
        ),
    )(q, k, v, rk, rv, seg.reshape(32, ROWS), w)


def solution(mesh):
    return jax.shard_map(
        on_device,
        mesh=mesh,
        in_specs=(
            P("blk", "head"),
            P("blk", "head"),
            P("blk", "head"),
            P("blk", "head"),
            P("blk", "head"),
            P(),
            P("head", "blk"),
        ),
        out_specs=P("blk", "head"),
        check_vma=False,
    )
```
